32 devices in a mesh: groups: 2 (over y), tile: 4 (over z), row: 4 (over x, core).
Axes of the slice: x: 2, y: 2, z: 4, core: 2. Of those that a mesh axis runs over, the one named last changes fastest.
Arguments:
- visibilities: float32 [2048, 128], P(('groups', 'tile', 'row')), parts along dimension 0, may hold values from -6 to 6
- uv_cells: float32 [2048, 128], P(('groups', 'tile', 'row')), parts along dimension 0, may hold values from 4 to 60
- block_owner: int32 [2048, 1], P(('groups', 'tile', 'row')), parts along dimension 0, may hold values from 0 to 15; in each aligned block of 64 rows (0 to 63, 64 to 127, ...) at most 12 rows name the same one
- block_subgrid: int32 [2048], P(('groups', 'tile', 'row')), parts along dimension 0, may hold values from 0 to 31
- block_count: int32 [2048], P(('groups', 'tile', 'row')), parts along dimension 0, may hold values from 1 to 64, 49152 in all
- block_stations: int32 [2048, 2], P(('groups', 'tile', 'row')), parts along dimension 0, may hold values from 0 to 511
- corners: int32 [1024, 2], P(('groups', 'tile', 'row')), parts along dimension 0, may hold values from 0 to 32767, as said below
- aterms: bfloat16 [512, 2, 4096], replicated, may hold values from -4.1875 to 4.1875
Outputs:
- spectrum: float32 [2, 8, 64, 32768], P(None, ('groups', 'row'), 'tile'), parts along dimension 1
The draws below stay inside these ranges and needn't reach their ends.
There are 2 independent parts, one for each index of `groups`. The reference program is written for one: setup_inputs(seed, part) draws one part's arguments, and reference() takes and returns one part's arrays. A program takes and returns all parts, laid end to end along the dimension named above; an argument that names none is the same for every part. Nothing has to cross between parts.
Inputs may be any that keep to these rules, and one draw needn't show every extreme that they name: `block_owner`: among the 64 blocks of one device at most 12 name one owner. Owner o holds subgrids o * 32 to o * 32 + 31; o counts the devices in the order of the joined tile and row axes. `corners`: subgrid s of owner o = t * 4 + r has its corner row in r * 64 to r * 64 + 63 and its corner column in t * 8192 to t * 8192 + 8191.
All inputs are finite; a program needn't handle non-finite values. No bound on the sum of `block_count` on one device may be relied on, other than what follows from the above.
Results may differ from the reference program's by a relative error of at most 0.0003.
Values sent between devices are 32-bit elements; how exact they have to be, the bound alone decides.
No kernel may reach another device: no remote copies, remote signals or barrier semaphores. Data moves between devices by JAX's collectives and lax.ppermute only.
A program may use at most 128 MiB of HBM per device.

```python
import math
import jax
import jax.numpy as jnp
import numpy as np
from jax import lax

SUB = 64
BV = 64
STATIONS = 512
GRID = 32768
SLAB = 256
NB_DEV = 64
SG_DEV = 32
OWNERS = 16
BLOCKS = 1024
SUBGRIDS = 512
CAP = 12
TR = 64
TC = 8192


def draw_corners(key, part):
    key = jax.random.fold_in(key, 7)
    stripes = SLAB // TR
    owner_index = jnp.arange(SUBGRIDS, dtype=jnp.int32) // SG_DEV
    tile_place = owner_index // stripes
    stripe_place = owner_index % stripes
    key_row, key_col = jax.random.split(key)
    row_offset = jax.random.randint(key_row, (SUBGRIDS,), 0, TR, dtype=jnp.int32)
    col_offset = jax.random.randint(key_col, (SUBGRIDS,), 0, TC, dtype=jnp.int32)
    row_offset = row_offset.at[0].set(0)
    col_offset = col_offset.at[0].set(0).at[SUBGRIDS - 1].set(TC - 1)
    return jnp.stack([stripe_place * TR + row_offset, tile_place * TC + col_offset], 1).astype(jnp.int32)


def set_ends(drawn, key, least, high):
    shape = drawn.shape
    spot = [jax.random.randint(jax.random.fold_in(key, axis), (), 0, shape[axis]) for axis in range(len(shape))]
    drawn = drawn.at[tuple(spot)].set(least)
    longest = shape.index(max(shape))
    spot[longest] = (spot[longest] + 1) % shape[longest]
    return drawn.at[tuple(spot)].set(high)


def steps_of(rng, extent, shards, low, largest):
    level = 1.0
    for dim, parts in shards:
        heights = jax.random.uniform(jax.random.fold_in(jax.random.fold_in(rng, 6), dim), (parts,), jnp.float32, low / len(shards), largest / len(shards))
        level = level * jnp.repeat(jnp.exp(heights), extent[dim] // parts).reshape((-1,) + (1,) * (len(extent) - 1 - dim))
    return level


def length_profile(number_of, total, limit, skew):
    portions = [(1 << 20) // math.isqrt(grade ** skew) + 1 for grade in range(2, number_of + 1)]
    surplus, given = total - limit - (number_of - 1), [1] * (number_of - 1)
    while surplus > 0:
        free = [i for i in range(number_of - 1) if given[i] < limit]
        mass, remaining = sum([portions[i] for i in free]), surplus
        for i in free:
            extra = min(limit - given[i], max(1, remaining * portions[i] // mass), surplus)
            given[i] = given[i] + extra
            surplus = surplus - extra
    return np.array([limit] + given)


def uneven_parts(rng, number_of, total, reach, lean):
    if number_of == 2:
        one = jax.random.randint(rng, (), max(1, total - reach), min(reach, total - 1) + 1)
        return jnp.stack([one, total - one])
    sizes = jnp.asarray(length_profile(number_of, total, reach, lean), jnp.int32)
    twos = (number_of - 1) // 2
    donor, receiver = sizes[1:1 + 2 * twos:2], sizes[2:2 + 2 * twos:2]
    room = jnp.minimum(donor - 1, reach - receiver)
    passed = jax.random.randint(jax.random.fold_in(rng, 1), (twos,), 0, 1 << 20) % (room + 1)
    sizes = sizes.at[1:1 + 2 * twos:2].set(donor - passed).at[2:2 + 2 * twos:2].set(receiver + passed)
    return sizes[jax.random.permutation(jax.random.fold_in(rng, 2), number_of)]


def deal_out(rng, own, number, rows, count, top, reach, skew):
    order = jax.random.permutation(rng, count)
    packed, usual = portions_of(count, rows * top, reach, skew, True), portions_of(count, rows * top, reach, skew, False)
    places = jnp.arange(count)

    def named(sizes, offset_by):
        used = int((sizes > 0).sum())
        fixed = max(1, used // 4)
        passed = fixed + (places - fixed + offset_by * (used - fixed)) % max(1, count - fixed)
        return jnp.zeros((count,), jnp.int32).at[order[jnp.where(places < fixed, places, passed)]].set(jnp.asarray(sizes, jnp.int32))

    sizes = jnp.where(number % 4 == 0, named(packed, number // 4), named(usual, number - number // 4 - 1))
    mixed = jax.random.permutation(jax.random.fold_in(own, 3), count)
    donor, taker = mixed[0:count // 2 * 2:2], mixed[1:count // 2 * 2:2]
    room = jnp.minimum(sizes[donor] - 1, reach - sizes[taker]) // 2
    room = jnp.where((donor == order[0]) | (taker == order[0]) | (sizes[taker] == 0), 0, jnp.maximum(room, 0))
    passed = jax.random.randint(jax.random.fold_in(own, 4), (count // 2,), 0, 1 << 20) % (room + 1)
    sizes = sizes.at[donor].add(-passed).at[taker].add(passed)
    items = jnp.searchsorted(jnp.cumsum(sizes), jnp.arange(rows * top), side="right").astype(jnp.int32)
    table = items.reshape(top, rows).T
    table = table[jax.random.permutation(jax.random.fold_in(own, 1), rows)]
    offset_by = jax.random.randint(jax.random.fold_in(own, 2), (rows, 1), 0, top)
    return jnp.take_along_axis(table, (jnp.arange(top)[None, :] + offset_by) % top, axis=1)


def portions_of(count, total, most, slope, full):
    weights = [(1 << 20) // math.isqrt(grade ** slope) + 1 for grade in range(1, count + 1)]
    largest = most if full else min(most, max(-(-total // count), total * weights[0] // sum(weights)))
    least = 1 if total - largest >= count - 1 else 0
    given, rest = [largest] + [least] * (count - 1), total - largest - least * (count - 1)
    while rest > 0:
        candidates = [i for i in range(1, count) if given[i] < largest] or [i for i in range(1, count) if given[i] < most]
        whole, remaining = sum([weights[i] for i in candidates]), rest
        for i in candidates:
            more = min(most - given[i], max(1, remaining * weights[i] // whole), rest)
            given[i] = given[i] + more
            rest = rest - more
    return np.array(given)


def normal_values(key, extent, deviation, most, cuts=(), held_as=jnp.bfloat16):
    entries = jax.random.normal(key, extent, jnp.float32) * deviation
    if len(cuts) > 0:
        entries = steps_of(key, extent, cuts, -0.22, 0.18) * entries
    return jnp.clip(entries, min=-most, max=most).astype(held_as)


def setup_inputs(seed: int = 0, part: int = 0) -> dict:
    streams_of = jax.random.split(jax.random.key(seed), 9)
    part_keys = jax.random.split(jax.random.fold_in(streams_of[8], part), 9)
    visibilities = normal_values(part_keys[0], (BLOCKS, 2 * BV), 1.0, 6.0, ((0, 16),), jnp.float32)
    uv_cells = jnp.clip(4.0 + 56.0 * jax.random.uniform(part_keys[1], (BLOCKS, 2 * BV), jnp.float32) ** steps_of(part_keys[1], (BLOCKS, 2 * BV), ((0, 16),), -0.2, 0.2), 4.0, 60.0)
    block_owner_keys = jax.random.split(jax.random.fold_in(part_keys[2], 1), BLOCKS // NB_DEV)
    block_owner_turns = jax.random.permutation(jax.random.fold_in(part_keys[2], 3), BLOCKS // NB_DEV)
    block_owner = jax.vmap(lambda own, number: deal_out(jax.random.fold_in(part_keys[2], 2), own, number, NB_DEV, OWNERS, 1, CAP, 2))(block_owner_keys, block_owner_turns).reshape((BLOCKS, 1))
    block_subgrid = set_ends(jax.random.randint(part_keys[3], (BLOCKS,), 0, SG_DEV), jax.random.fold_in(part_keys[3], 1), 0, SG_DEV - 1).astype(jnp.int32)
    block_count = uneven_parts(part_keys[4], BLOCKS, BLOCKS * BV * 3 // 4, BV, 1).astype(jnp.int32)
    block_stations = set_ends(jax.random.randint(part_keys[5], (BLOCKS, 2), 0, STATIONS), jax.random.fold_in(part_keys[5], 1), 0, STATIONS - 1).astype(jnp.int32)
    corners = draw_corners(jax.random.fold_in(jax.random.fold_in(streams_of[8], part), 71), part)
    aterms = normal_values(streams_of[7], (STATIONS, 2, SUB * SUB), 0.7, 4.1875)
    return {"visibilities": visibilities, "uv_cells": uv_cells, "block_owner": block_owner, "block_subgrid": block_subgrid, "block_count": block_count, "block_stations": block_stations, "corners": corners, "aterms": aterms}


def grid_blocks(payload, labels, aterms, side):
    per_block = payload.shape[1] // 4
    vis_re = payload[:, :per_block]
    vis_im = payload[:, per_block:2 * per_block]
    coord_u = payload[:, 2 * per_block:3 * per_block]
    coord_v = payload[:, 3 * per_block:]
    live = (jnp.arange(per_block, dtype=jnp.int32)[None, :] < labels[:, 1:2]).astype(jnp.float32) / math.sqrt(per_block)
    cells = jnp.arange(side).astype(jnp.float32)
    phase_u = 2.0 * math.pi / side * coord_u[:, :, None] * cells[None, None, :]
    phase_v = 2.0 * math.pi / side * coord_v[:, :, None] * cells[None, None, :]
    weight_re = (vis_re * live)[:, :, None]
    weight_im = (vis_im * live)[:, :, None]
    cos_u = jnp.cos(phase_u)
    sin_u = jnp.sin(phase_u)
    left_re = weight_re * cos_u - weight_im * sin_u
    left_im = weight_re * sin_u + weight_im * cos_u
    cos_v = jnp.cos(phase_v)
    sin_v = jnp.sin(phase_v)
    high = lax.Precision.HIGHEST
    image_re = jnp.einsum('gkl,gkm->glm', left_re, cos_v, precision=high) - jnp.einsum('gkl,gkm->glm', left_im, sin_v, precision=high)
    image_im = jnp.einsum('gkl,gkm->glm', left_re, sin_v, precision=high) + jnp.einsum('gkl,gkm->glm', left_im, cos_v, precision=high)
    count = payload.shape[0]
    image_re = image_re.reshape(count, side * side)
    image_im = image_im.reshape(count, side * side)
    edge = (2.0 * cells + 1.0) / side - 1.0
    taper = 1.0 - 0.9 * edge * edge
    taper_two = (taper[:, None] * taper[None, :]).reshape(side * side)
    first_gain = jnp.take(aterms, labels[:, 2], axis=0).astype(jnp.float32)
    second_gain = jnp.take(aterms, labels[:, 3], axis=0).astype(jnp.float32)
    factor_re = (first_gain[:, 0] * second_gain[:, 0] + first_gain[:, 1] * second_gain[:, 1]) * taper_two
    factor_im = (first_gain[:, 1] * second_gain[:, 0] - first_gain[:, 0] * second_gain[:, 1]) * taper_two
    out_re = image_re * factor_re - image_im * factor_im
    out_im = image_re * factor_im + image_im * factor_re
    return jnp.stack([out_re, out_im], 1)

def reference(visibilities, uv_cells, block_owner, block_subgrid, block_count, block_stations, corners, aterms):
    payload = jnp.concatenate([visibilities, uv_cells], 1)
    labels = jnp.stack([block_subgrid, block_count, block_stations[:, 0], block_stations[:, 1]], 1).astype(jnp.int32)
    target = (block_owner[:, 0] * SG_DEV + block_subgrid).astype(jnp.int32)
    batch_rows = 128 if BLOCKS % 128 == 0 else BLOCKS
    batches = BLOCKS // batch_rows
    payload_b = payload.reshape(batches, batch_rows, payload.shape[1])
    labels_b = labels.reshape(batches, batch_rows, 4)
    target_b = target.reshape(batches, batch_rows)

    def add_batch(running, pieces):
        weighted = grid_blocks(pieces[0], pieces[1], aterms, SUB)
        return (running.at[pieces[2]].add(weighted), None)
    start_sub = jnp.zeros((SUBGRIDS, 2, SUB * SUB), jnp.float32)
    subgrid, _ = lax.scan(add_batch, start_sub, (payload_b, labels_b, target_b))
    subgrid = subgrid.reshape(SUBGRIDS, 2, SUB, SUB)
    patch = jnp.fft.fft2(lax.complex(subgrid[:, 0], subgrid[:, 1])) / SUB
    uv_patch = jnp.stack([jnp.real(patch), jnp.imag(patch)], 0).astype(jnp.float32)
    padded = jnp.zeros((2, SLAB + SUB, GRID + SUB), jnp.float32)

    def place(index, canvas):
        row_at = corners[index, 0].astype(jnp.int32)
        col_at = corners[index, 1].astype(jnp.int32)
        zero_at = jnp.zeros((), jnp.int32)
        current = lax.dynamic_slice(canvas, (zero_at, row_at, col_at), (2, SUB, SUB))
        return lax.dynamic_update_slice(canvas, current + uv_patch[:, index], (zero_at, row_at, col_at))
    padded = lax.fori_loop(0, SUBGRIDS, place, padded)
    grid = padded[:, :SLAB, :GRID]
    grid = grid.at[:, :, :SUB].add(padded[:, :SLAB, GRID:])
    spectrum = jnp.fft.fft(lax.complex(grid[0], grid[1]), axis=1) / math.sqrt(GRID)
    result = jnp.stack([jnp.real(spectrum), jnp.imag(spectrum)], 0).astype(jnp.float32)
    return result.reshape(2, SLAB // TR, TR, GRID)
```

```python
import functools
import math

import jax
import jax.numpy as jnp
import numpy as np
from jax import lax
from jax.experimental import pallas as pl
from jax.experimental.pallas import tpu as pltpu
from jax.sharding import PartitionSpec as P

GRID = 32768
SLAB = 256
SIDE = 64
LANES = 128
UNROLL = 4
HALF = GRID // SIDE // 2

SIN_TERMS = (
    6.2831852724479385, -41.3416970381994, 81.60502363801741, -76.70153767001833,
    42.01607576032372, -14.868322746301509, 3.199338837237415,
)
COS_TERMS = (
    0.9999999890590211, -19.73920449945394, 64.93911745989672, -85.45013953089433,
    60.167630950968515, -25.967599248305554, 6.528658160795414,
)


def poly(terms, z):
    total = jnp.full_like(z, terms[-1])
    for term in terms[-2::-1]:
        total = total * z + term
    return total


def cos_sin(turns):
    rest = turns - jnp.round(turns)
    z = rest * rest
    return poly(COS_TERMS, z), rest * poly(SIN_TERMS, z)


def split(x):
    high = x.astype(jnp.bfloat16)
    return high, (x - high.astype(jnp.float32)).astype(jnp.bfloat16)


def split_table(table):
    high = table.astype(jnp.bfloat16)
    return high, (table - high.astype(np.float64)).astype(jnp.bfloat16)


def dot(a, b):
    return jnp.dot(a, b, preferred_element_type=jnp.float32)


def dot_nt(a, b):
    return lax.dot_general(a, b, (((1,), (1,)), ((), ())), preferred_element_type=jnp.float32)


def taper():
    edge = (2.0 * np.arange(SIDE) + 1.0) / SIDE - 1.0
    return 1.0 - 0.9 * edge * edge


def column_table():
    m = np.arange(SIDE)
    angle = 2.0 * np.pi * (m[:, None] * m[None, :] % SIDE) / SIDE
    scale = 1.0 / (SIDE * math.sqrt(SIDE) * math.sqrt(GRID))
    real = scale * taper()[:, None] * np.cos(angle)
    imag = -scale * taper()[:, None] * np.sin(angle)
    table = np.zeros((2, 2, SIDE, 2, 2, 2, SIDE))
    for p in range(2):
        table[0, p, :, 0, p, 0] = real
        table[0, p, :, 0, p, 1] = imag
        table[1, p, :, 0, p, 0] = -imag
        table[1, p, :, 0, p, 1] = real
        table[0, p, :, 1, p, 0] = -imag
        table[0, p, :, 1, p, 1] = real
        table[1, p, :, 1, p, 0] = -real
        table[1, p, :, 1, p, 1] = -imag
    return table.reshape(4 * SIDE, 8 * SIDE)


def row_table():
    rho = np.arange(2 * SIDE) % SIDE
    a = np.arange(SIDE // 2)
    blocks = []
    for kind in (np.cos, lambda t: -np.sin(t)):
        for p in range(2):
            l = 2 * a + p
            blocks.append(taper()[l][None, :] * kind(2.0 * np.pi * (rho[:, None] * l[None, :] % SIDE) / SIDE))
    high, low = split_table(np.concatenate(blocks, 1))
    return np.concatenate([high, low, high], 1)


def stage_tables():
    k = np.arange(HALF)[:, None]
    t = np.arange(HALF)[None, :]
    out = []
    for p in range(2):
        angle = 2.0 * np.pi * (k * (2 * t + p) % (2 * HALF)) / (2 * HALF)
        high, low = split_table(np.concatenate([np.cos(angle), -np.sin(angle)], 1))
        out.append(np.concatenate([high, low], 0))
    return out


def twiddle_tables():
    k = np.arange(2 * HALF)[:, None]
    kappa = np.arange(SIDE)[None, :]
    angle = 2.0 * np.pi * (k * kappa % GRID) / GRID
    c, s = np.cos(angle), np.sin(angle)
    return (
        np.concatenate([c, c], 1).astype(np.float32),
        np.concatenate([s, -s], 1).astype(np.float32),
    )


def last_table():
    k = np.arange(SIDE)[:, None]
    kappa = np.arange(SIDE)[None, :]
    angle = 2.0 * np.pi * (k * kappa % SIDE) / SIDE
    c, s = np.cos(angle), np.sin(angle)
    high, low = split_table(np.block([[c, s], [-s, c]]))
    return np.concatenate([high, low], 0)


def pack_kernel(capacity, stride, owner, sub, count, stations, corners, vis, uv, message, used):
    owners = message.shape[0] // (2 * stride)
    blocks = vis.shape[0]
    lane = lax.broadcasted_iota(jnp.int32, (1, LANES), 1)
    message[...] = jnp.zeros_like(message)

    def corner(i, row):
        return jnp.where(lane == i, corners[i].astype(jnp.float32), row)

    corner_row = lax.fori_loop(0, corners.shape[0], corner, jnp.zeros((1, LANES), jnp.float32), unroll=8)

    def clear(o, carry):
        used[o] = 0
        message[pl.ds((2 * o + 1) * stride + capacity, 1), :] = corner_row
        return carry

    lax.fori_loop(0, owners, clear, 0, unroll=8)

    def place(g, carry):
        o = owner[g]
        slot = used[o]
        used[o] = slot + 1
        row = 2 * o * stride + slot
        live = (lane % SIDE) < count[g]
        message[pl.ds(row, 1), :] = jnp.where(live, vis[pl.ds(g, 1), :], 0.0)
        message[pl.ds(row + stride, 1), :] = uv[pl.ds(g, 1), :]
        tags_at = pl.ds(2 * o * stride + capacity, 1)
        tag_row = message[tags_at, :]
        at = 4 * slot
        for i, value in enumerate((sub[g], count[g], stations[2 * g], stations[2 * g + 1])):
            tag_row = jnp.where(lane == at + i, value.astype(jnp.float32), tag_row)
        message[tags_at, :] = tag_row
        return carry

    lax.fori_loop(0, blocks, place, 0, unroll=4)


def grid_kernel(
    capacity, stride, pieces, tags, got, aterms, col_high, col_low, rows, *refs
):
    outs, (rows_v, rows_uv, left, right_re, right_im, two_u, two_v, subgrids, listed) = (
        refs[:pieces],
        refs[pieces:],
    )
    owners = got.shape[0] // (2 * stride)
    sub_count = outs[0].shape[0]
    piece_rows = outs[0].shape[1]
    room = rows_v.shape[0]
    lane = lax.broadcasted_iota(jnp.int32, (1, LANES), 1)
    low = lane < SIDE
    tag_width = 2 * LANES
    tile_at, row_at = lax.axis_index("tile"), lax.axis_index("row")
    mine = (tile_at * lax.axis_size("row") + row_at) * tag_width + LANES

    subgrids[...] = jnp.zeros_like(subgrids)

    def collect(source, found):
        for c in range(capacity):
            listed[found] = 2 * source * stride + c
            found = found + (tags[source * tag_width + 4 * c + 1] > 0).astype(jnp.int32)
        return found

    total = lax.fori_loop(0, owners, collect, jnp.int32(0))
    for i in range(8):
        listed[total + i] = capacity + 1

    def fetch(n, carry):
        for e in range(8):
            at = n * 8 + e
            entry = listed[at]
            source, c = entry // (2 * stride), entry % stride
            sub = tags[source * tag_width + 4 * c]
            shift_u = (tags[mine + 2 * sub] & (SIDE - 1)).astype(jnp.float32)
            shift_v = (tags[mine + 2 * sub + 1] & (SIDE - 1)).astype(jnp.float32)
            rows_v[pl.ds(at, 1), :] = got[pl.ds(entry, 1), :]
            rows_uv[pl.ds(at, 1), :] = got[pl.ds(entry + stride, 1), :] + jnp.where(low, shift_u, shift_v)
        base = pl.multiple_of(n * 8, 8)
        v = rows_v[pl.ds(base, 8), :]
        turns = rows_uv[pl.ds(base, 8), :] * (1.0 / SIDE)
        c1, s1 = cos_sin(turns)
        c16, s16 = cos_sin(turns * 16.0)
        rc1, rs1 = pltpu.roll(c1, SIDE, 1), pltpu.roll(s1, SIDE, 1)
        rc16, rs16 = pltpu.roll(c16, SIDE, 1), pltpu.roll(s16, SIDE, 1)
        cu, su = jnp.where(low, c1, rc1), jnp.where(low, s1, rs1)
        cv, sv = jnp.where(low, rc1, c1), jnp.where(low, rs1, s1)
        cu16, su16 = jnp.where(low, c16, rc16), jnp.where(low, s16, rs16)
        cv16, sv16 = jnp.where(low, rc16, c16), jnp.where(low, rs16, s16)
        two_u[pl.ds(base, 8), :] = 2.0 * cu16
        two_v[pl.ds(base, 8), :] = 2.0 * cv16
        a = v
        b = pltpu.roll(v, SIDE, 1) * jnp.where(low, -1.0, 1.0)
        x = jnp.broadcast_to(jnp.where(low, 1.0, 0.0), v.shape)
        y = jnp.broadcast_to(jnp.where(low, 0.0, 1.0), v.shape)
        for l in range(16):
            left[pl.ds(l * room + base, 8), :] = a
            left[pl.ds((l + 16) * room + base, 8), :] = a * cu16 + b * su16
            right_re[pl.ds(l * room + base, 8), :] = x
            right_im[pl.ds(l * room + base, 8), :] = y
            right_re[pl.ds((l + 16) * room + base, 8), :] = x * cv16 - y * sv16
            right_im[pl.ds((l + 16) * room + base, 8), :] = y * cv16 + x * sv16
            if l < 15:
                a, b = a * cu + b * su, b * cu - a * su
                x, y = x * cv - y * sv, y * cv + x * sv
        return carry

    lax.fori_loop(0, (total + 7) // 8, fetch, 0)

    def image(at):
        ku = two_u[pl.ds(at, 1), :]
        kv = two_v[pl.ds(at, 1), :]
        ls = []
        for p in range(2):
            chain = [left[pl.ds((16 * j + p) * room + at, 8, stride=2 * room), :] for j in range(2)]
            for j in range(2):
                chain.append(ku * chain[-1] - chain[-2])
            ls.extend(chain)
        sides = []
        for ref in (right_re, right_im):
            chain = [ref[pl.ds(8 * q * room + at, 8, stride=room), :] for q in range(4)]
            for q in range(4):
                chain.append(kv * chain[-2] - chain[-4])
            sides.append(jnp.concatenate(chain, 0))
        l_high, l_low = split(jnp.concatenate(ls, 0))
        re_high, re_low = split(sides[0])
        im_high, im_low = split(sides[1])
        r_high = jnp.concatenate([re_high, re_high, im_high, im_high], 0)
        r_low = jnp.concatenate([re_low, re_low, im_low, im_low], 0)
        both = dot_nt(
            jnp.concatenate([l_high, l_low, l_high], 1), jnp.concatenate([r_high, r_high, r_low], 1)
        )
        half = SIDE // 2
        re = jnp.where(low, both[:half, :LANES], both[half:, :LANES])
        im = jnp.where(low, both[:half, LANES:], both[half:, LANES:])
        return re, im

    def weigh(turn, carry):
        half = SIDE // 2
        for e in range(UNROLL):
            at = turn * UNROLL + e
            entry = listed[at]
            source, c = entry // (2 * stride), entry % stride
            tag = source * tag_width + 4 * c
            sub, first, second = tags[tag], tags[tag + 2], tags[tag + 3]
            re, im = image(at)
            gain_p = aterms[first].astype(jnp.float32)
            gain_q = aterms[second].astype(jnp.float32)
            pr, pi = gain_p[:half], gain_p[half:]
            qr, qi = gain_q[:half], gain_q[half:]
            fr = pr * qr + pi * qi
            fi = pi * qr - pr * qi
            subgrids[sub, :half, :] += re * fr - im * fi
            subgrids[sub, half:, :] += re * fi + im * fr
        return carry

    lax.fori_loop(0, (total + UNROLL - 1) // UNROLL, weigh, 0)

    batch = min(8, sub_count)

    def transform(turn, carry):
        half = SIDE // 2
        first = turn * batch
        data = []
        for e in range(batch):
            both = subgrids[first + e]
            data.append(jnp.concatenate([both[:half], both[half:]], 1))
        d_high, d_low = split(jnp.concatenate(data, 0))
        mid = dot(d_high, col_high[...]) + dot(d_low, col_high[...]) + dot(d_high, col_low[...])
        table = rows[...]
        for e in range(batch):
            part = mid[e * half : (e + 1) * half]
            stack = jnp.concatenate([part[:, q * LANES : (q + 1) * LANES] for q in range(4)], 0)
            s_high, s_low = split(stack)
            patch = dot(table, jnp.concatenate([s_high, s_high, s_low], 0))
            for k in range(pieces):
                outs[k][first + e] = patch[k * piece_rows : (k + 1) * piece_rows]
        return carry

    lax.fori_loop(0, sub_count // batch, transform, 0)


def spectrum_kernel(
    pieces, stripe_rows, tags, *refs
):
    own, below = refs[:pieces], refs[pieces : 2 * pieces]
    first0, first1, turn_c, turn_s, last, out, grid = refs[2 * pieces :]
    sub_count, piece_rows, _ = own[0].shape
    tag_width = 2 * LANES
    blocks = 2 * HALF
    tile_at, row_at = lax.axis_index("tile"), lax.axis_index("row")
    row_count = lax.axis_size("row")
    lane = lax.broadcasted_iota(jnp.int32, (1, LANES), 1)
    sign = jnp.where(lane < SIDE, -1.0, 1.0)

    @pl.when(pl.program_id(0) == 0)
    def _():
        grid[...] = jnp.zeros_like(grid)
        kappa = lax.broadcasted_iota(jnp.int32, (piece_rows, LANES), 1) % SIDE
        rho = lax.broadcasted_iota(jnp.int32, (piece_rows, LANES), 0) + piece_rows * tile_at
        above = jnp.maximum(row_at - 1, 0)

        def add(ref, base, stripe, keep_late, s):
            corner_row = tags[base + 2 * s]
            corner_col = tags[base + 2 * s + 1]
            offset = corner_row - stripe * stripe_rows
            keep = (rho >= offset) if keep_late else (rho < offset)
            piece = jnp.where(keep, ref[s], 0.0)
            block = corner_col // SIDE
            ahead = jnp.where(kappa >= corner_col % SIDE, piece, 0.0)
            here = pl.multiple_of(block * piece_rows, piece_rows)
            grid[pl.ds(here, piece_rows), :] += ahead
            there = pl.multiple_of(((block + 1) % blocks) * piece_rows, piece_rows)
            grid[pl.ds(there, piece_rows), :] += piece - ahead

        for k in range(pieces):
            source = (tile_at - k + pieces) % pieces
            for ref, stripe, keep_late in ((own[k], row_at, True), (below[k], above, False)):
                base = (source * row_count + stripe) * tag_width + LANES

                def body(s, carry, ref=ref, base=base, stripe=stripe, keep_late=keep_late):
                    add(ref, base, stripe, keep_late, s)
                    return carry

                lax.fori_loop(0, sub_count, body, 0, unroll=4)

    rows_here = out.shape[2] // (4 * SIDE)

    def pair(index, carry):
        outs = []
        for p, table in ((0, first0), (1, first1)):
            cols, turned = [], []
            for e in range(2):
                row = pl.program_id(0) * rows_here + 2 * index + e
                x = grid[pl.ds(p * piece_rows + row, HALF, stride=2 * piece_rows), :]
                cols.append(x)
                turned.append(pltpu.roll(x, SIDE, 1) * sign)
            data = jnp.concatenate([jnp.concatenate(cols, 1), jnp.concatenate(turned, 1)], 0)
            high, low = split(data)
            top = dot(table[...], high)
            outs.append(top[:HALF] + top[HALF:] + dot(table[:HALF, :], low))
        halves = (outs[0] + outs[1], outs[0] - outs[1])
        for e in range(2):
            parts = []
            for h in range(2):
                y = halves[h][:, e * LANES : (e + 1) * LANES]
                at = pl.ds(h * HALF, HALF)
                parts.append(y * turn_c[at, :] + pltpu.roll(y, SIDE, 1) * turn_s[at, :])
            high, low = split(jnp.concatenate(parts, 0))
            top = dot_nt(last[...], high)
            z = top[:LANES] + top[LANES:] + dot_nt(last[:LANES, :], low)
            for c in range(2):
                for q in range(4):
                    begin = q * rows_here + 2 * index + e
                    out[c, 0, pl.ds(begin, SIDE, stride=4 * rows_here), :] = z[
                        c * SIDE : (c + 1) * SIDE, q * LANES : (q + 1) * LANES
                    ]
        return carry

    lax.fori_loop(0, rows_here // 2, pair, 0)


def local(
    visibilities, uv_cells, block_owner, block_subgrid, block_count, block_stations, corners, aterms
):
    tile_count = lax.axis_size("tile")
    row_count = lax.axis_size("row")
    owner_count = tile_count * row_count
    blocks_here = visibilities.shape[0]
    sub_count = corners.shape[0]
    stations = aterms.shape[0]
    capacity = max(2, 3 * blocks_here // owner_count)
    stride = 8 * (-(-(capacity + 2) // 8))
    stripe_rows = SLAB // row_count
    piece_rows = stripe_rows // tile_count
    smem = pl.BlockSpec(memory_space=pltpu.SMEM)
    vmem = pl.BlockSpec(memory_space=pltpu.VMEM)

    message = pl.pallas_call(
        functools.partial(pack_kernel, capacity, stride),
        out_shape=jax.ShapeDtypeStruct((2 * owner_count * stride, LANES), jnp.float32),
        in_specs=[smem] * 5 + [vmem] * 2,
        out_specs=vmem,
        scratch_shapes=[pltpu.SMEM((owner_count,), jnp.int32)],
        name="pack",
    )(
        block_owner.reshape(-1),
        block_subgrid,
        block_count,
        block_stations.reshape(-1),
        corners.reshape(-1),
        visibilities,
        uv_cells,
    )
    got = lax.all_to_all(
        message.reshape(owner_count, 2, stride, LANES),
        ("tile", "row"),
        split_axis=0,
        concat_axis=0,
        tiled=True,
    )
    tags = got[:, :, capacity, :].astype(jnp.int32).reshape(-1)
    got = got.reshape(2 * owner_count * stride, LANES)

    gains = aterms.reshape(stations, 2 * aterms.shape[2] // LANES, LANES)
    col_high, col_low = split_table(column_table())
    window = lax.dynamic_slice(
        jnp.asarray(row_table()), (piece_rows * lax.axis_index("tile"), 0), (SIDE, 6 * SIDE)
    )
    room = owner_count * capacity + 8
    patches = pl.pallas_call(
        functools.partial(grid_kernel, capacity, stride, tile_count),
        out_shape=[
            jax.ShapeDtypeStruct((sub_count, piece_rows, LANES), jnp.float32)
            for _ in range(tile_count)
        ],
        in_specs=[smem] + [vmem] * 5,
        out_specs=[vmem] * tile_count,
        scratch_shapes=[
            pltpu.VMEM((room, LANES), jnp.float32),
            pltpu.VMEM((room, LANES), jnp.float32),
            pltpu.VMEM((32 * room, LANES), jnp.float32),
            pltpu.VMEM((32 * room, LANES), jnp.float32),
            pltpu.VMEM((32 * room, LANES), jnp.float32),
            pltpu.VMEM((room, LANES), jnp.float32),
            pltpu.VMEM((room, LANES), jnp.float32),
            pltpu.VMEM((sub_count, SIDE, LANES), jnp.float32),
            pltpu.SMEM((room + 8,), jnp.int32),
        ],
        compiler_params=pltpu.CompilerParams(vmem_limit_bytes=48 * 1024 * 1024),
        name="gridding",
    )(tags, got, gains, col_high, col_low, window)

    own, below = [], []
    down = [(i, i + 1) for i in range(row_count - 1)]
    for k in range(tile_count):
        piece = patches[k]
        if k > 0:
            piece = lax.ppermute(piece, "tile", [(i, (i + k) % tile_count) for i in range(tile_count)])
        own.append(piece)
        below.append(lax.ppermute(piece, "row", down))

    first0, first1 = stage_tables()
    turn_c, turn_s = twiddle_tables()
    rows_here = min(8, piece_rows)
    steps = piece_rows // rows_here
    depth = rows_here * GRID // LANES
    spectrum = pl.pallas_call(
        functools.partial(spectrum_kernel, tile_count, stripe_rows),
        grid=(steps,),
        out_shape=jax.ShapeDtypeStruct((2, steps, depth, LANES), jnp.float32),
        in_specs=[smem] + [vmem] * (2 * tile_count + 5),
        out_specs=pl.BlockSpec((2, 1, depth, LANES), lambda i: (0, i, 0, 0)),
        scratch_shapes=[pltpu.VMEM((2 * HALF * piece_rows, LANES), jnp.float32)],
        compiler_params=pltpu.CompilerParams(vmem_limit_bytes=48 * 1024 * 1024),
        name="spectrum",
    )(tags, *own, *below, first0, first1, turn_c, turn_s, last_table())
    spectrum = spectrum.reshape(2, steps, GRID // LANES, rows_here, LANES).transpose(0, 1, 3, 2, 4)
    return spectrum.reshape(2, 1, piece_rows, GRID)


def solution(mesh):
    in_specs = (
        P(("groups", "tile", "row"), None),
        P(("groups", "tile", "row"), None),
        P(("groups", "tile", "row"), None),
        P(("groups", "tile", "row")),
        P(("groups", "tile", "row")),
        P(("groups", "tile", "row"), None),
        P(("groups", "tile", "row"), None),
        P(),
    )
    out_specs = P(None, ("groups", "row"), "tile", None)
    return jax.shard_map(local, mesh=mesh, in_specs=in_specs, out_specs=out_specs, check_vma=False)
```

```python
import functools
import math

import jax
import jax.numpy as jnp
import numpy as np
from jax import lax
from jax.experimental import pallas as pl
from jax.experimental.pallas import tpu as pltpu
from jax.sharding import PartitionSpec as P

GRID = 32768
SLAB = 256
SIDE = 64
LANES = 128
UNROLL = 16
PARTS = 8
HALF = GRID // SIDE // 2

SIN_TERMS = (
    6.2831852724479385, -41.3416970381994, 81.60502363801741, -76.70153767001833,
    42.01607576032372, -14.868322746301509, 3.199338837237415,
)
COS_TERMS = (
    0.9999999890590211, -19.73920449945394, 64.93911745989672, -85.45013953089433,
    60.167630950968515, -25.967599248305554, 6.528658160795414,
)


def poly(terms, z):
    total = jnp.full_like(z, terms[-1])
    for term in terms[-2::-1]:
        total = total * z + term
    return total


def cos_sin(turns):
    rest = turns - jnp.round(turns)
    z = rest * rest
    return poly(COS_TERMS, z), rest * poly(SIN_TERMS, z)


def split(x):
    high = x.astype(jnp.bfloat16)
    return high, (x - high.astype(jnp.float32)).astype(jnp.bfloat16)


def split_table(table):
    high = table.astype(jnp.bfloat16)
    return high, (table - high.astype(np.float64)).astype(jnp.bfloat16)


def dot(a, b):
    return jnp.dot(a, b, preferred_element_type=jnp.float32)


def dot_nt(a, b):
    return lax.dot_general(a, b, (((1,), (1,)), ((), ())), preferred_element_type=jnp.float32)


def taper():
    edge = (2.0 * np.arange(SIDE) + 1.0) / SIDE - 1.0
    return 1.0 - 0.9 * edge * edge


def column_table():
    m = np.arange(SIDE)
    angle = 2.0 * np.pi * (m[:, None] * m[None, :] % SIDE) / SIDE
    scale = 1.0 / (SIDE * math.sqrt(SIDE) * math.sqrt(GRID))
    real = scale * taper()[:, None] * np.cos(angle)
    imag = -scale * taper()[:, None] * np.sin(angle)
    table = np.zeros((2, 2, SIDE, 2, 2, 2, SIDE))
    for p in range(2):
        table[0, p, :, 0, p, 0] = real
        table[0, p, :, 0, p, 1] = imag
        table[1, p, :, 0, p, 0] = -imag
        table[1, p, :, 0, p, 1] = real
        table[0, p, :, 1, p, 0] = -imag
        table[0, p, :, 1, p, 1] = real
        table[1, p, :, 1, p, 0] = -real
        table[1, p, :, 1, p, 1] = -imag
    return table.reshape(4 * SIDE, 8 * SIDE)


def row_table():
    rho = np.arange(2 * SIDE) % SIDE
    a = np.arange(SIDE // 2)
    blocks = []
    for kind in (np.cos, lambda t: -np.sin(t)):
        for p in range(2):
            l = 2 * a + p
            blocks.append(taper()[l][None, :] * kind(2.0 * np.pi * (rho[:, None] * l[None, :] % SIDE) / SIDE))
    high, low = split_table(np.concatenate(blocks, 1))
    return np.concatenate([high, low, high], 1)


def stage_tables():
    k = np.arange(HALF)[:, None]
    t = np.arange(HALF)[None, :]
    out = []
    for p in range(2):
        angle = 2.0 * np.pi * (k * (2 * t + p) % (2 * HALF)) / (2 * HALF)
        high, low = split_table(np.concatenate([np.cos(angle), -np.sin(angle)], 1))
        out.append(np.concatenate([high, low], 0))
    return out


def twiddle_tables():
    k = np.arange(2 * HALF)[:, None]
    kappa = np.arange(SIDE)[None, :]
    angle = 2.0 * np.pi * (k * kappa % GRID) / GRID
    c, s = np.cos(angle), np.sin(angle)
    return (
        np.concatenate([c, c], 1).astype(np.float32),
        np.concatenate([s, -s], 1).astype(np.float32),
    )


def last_table():
    k = np.arange(SIDE)[:, None]
    kappa = np.arange(SIDE)[None, :]
    angle = 2.0 * np.pi * (k * kappa % SIDE) / SIDE
    c, s = np.cos(angle), np.sin(angle)
    high, low = split_table(np.block([[c, s], [-s, c]]))
    return np.concatenate([high, low], 0)


def pack_kernel(capacity, stride, owner, sub, count, stations, corners, vis, uv, message, used):
    owners = message.shape[0] // (2 * stride)
    blocks = vis.shape[0]
    lane = lax.broadcasted_iota(jnp.int32, (1, LANES), 1)
    message[...] = jnp.zeros_like(message)

    def corner(i, row):
        return jnp.where(lane == i, corners[i % 2, i // 2].astype(jnp.float32), row)

    corner_row = lax.fori_loop(0, 2 * corners.shape[1], corner, jnp.zeros((1, LANES), jnp.float32), unroll=8)

    def clear(o, carry):
        used[o] = 0
        message[pl.ds((2 * o + 1) * stride + capacity, 1), :] = corner_row
        return carry

    lax.fori_loop(0, owners, clear, 0, unroll=8)

    def place(g, carry):
        o = owner[g]
        slot = used[o]
        used[o] = slot + 1
        row = 2 * o * stride + slot
        live = (lane % SIDE) < count[g]
        message[pl.ds(row, 1), :] = jnp.where(live, vis[pl.ds(g, 1), :], 0.0)
        message[pl.ds(row + stride, 1), :] = uv[pl.ds(g, 1), :]
        tags_at = pl.ds(2 * o * stride + capacity, 1)
        tag_row = message[tags_at, :]
        at = 4 * slot
        for i, value in enumerate((sub[g], count[g], stations[0, g], stations[1, g])):
            tag_row = jnp.where(lane == at + i, value.astype(jnp.float32), tag_row)
        message[tags_at, :] = tag_row
        return carry

    lax.fori_loop(0, blocks, place, 0, unroll=4)


def grid_kernel(
    capacity, stride, pieces, tags, got, aterms, col_high, col_low, rows, *refs
):
    outs, (rows_v, rows_uv, left, right_re, right_im, two_u, two_v, subgrids, raw, gains, listed, arrived) = (
        refs[:pieces],
        refs[pieces:],
    )
    owners = got.shape[0] // (2 * stride)
    sub_count = outs[0].shape[0]
    piece_rows = outs[0].shape[1]
    room = rows_v.shape[0]
    lane = lax.broadcasted_iota(jnp.int32, (1, LANES), 1)
    low = lane < SIDE
    tag_width = 2 * LANES
    tile_at, row_at = lax.axis_index("tile"), lax.axis_index("row")
    mine = (tile_at * lax.axis_size("row") + row_at) * tag_width + LANES

    part = aterms.shape[0] // PARTS
    loads = [
        pltpu.make_async_copy(
            aterms.at[pl.ds(i * part, part)], raw.at[pl.ds(i * part, part)], arrived.at[i]
        )
        for i in range(PARTS)
    ]
    for load in loads:
        load.start()
    subgrids[...] = jnp.zeros_like(subgrids)

    def collect(source, found):
        for c in range(capacity):
            listed[found] = 2 * source * stride + c
            found = found + (tags[source * tag_width + 4 * c + 1] > 0).astype(jnp.int32)
        return found

    total = lax.fori_loop(0, owners, collect, jnp.int32(0))
    for i in range(UNROLL):
        listed[total + i] = capacity + 1

    def fetch(n, carry):
        for e in range(8):
            at = n * 8 + e
            entry = listed[at]
            source, c = entry // (2 * stride), entry % stride
            sub = tags[source * tag_width + 4 * c]
            shift_u = (tags[mine + 2 * sub] & (SIDE - 1)).astype(jnp.float32)
            shift_v = (tags[mine + 2 * sub + 1] & (SIDE - 1)).astype(jnp.float32)
            rows_v[pl.ds(at, 1), :] = got[pl.ds(entry, 1), :]
            rows_uv[pl.ds(at, 1), :] = got[pl.ds(entry + stride, 1), :] + jnp.where(low, shift_u, shift_v)
        base = pl.multiple_of(n * 8, 8)
        v = rows_v[pl.ds(base, 8), :]
        turns = rows_uv[pl.ds(base, 8), :] * (1.0 / SIDE)
        c1, s1 = cos_sin(turns)
        c16, s16 = cos_sin(turns * 16.0)
        rc1, rs1 = pltpu.roll(c1, SIDE, 1), pltpu.roll(s1, SIDE, 1)
        rc16, rs16 = pltpu.roll(c16, SIDE, 1), pltpu.roll(s16, SIDE, 1)
        cu, su = jnp.where(low, c1, rc1), jnp.where(low, s1, rs1)
        cv, sv = jnp.where(low, rc1, c1), jnp.where(low, rs1, s1)
        cu16, su16 = jnp.where(low, c16, rc16), jnp.where(low, s16, rs16)
        cv16, sv16 = jnp.where(low, rc16, c16), jnp.where(low, rs16, s16)
        two_u[pl.ds(base, 8), :] = 2.0 * cu16
        two_v[pl.ds(base, 8), :] = 2.0 * cv16
        a = v
        b = pltpu.roll(v, SIDE, 1) * jnp.where(low, -1.0, 1.0)
        x = jnp.broadcast_to(jnp.where(low, 1.0, 0.0), v.shape)
        y = jnp.broadcast_to(jnp.where(low, 0.0, 1.0), v.shape)
        for l in range(16):
            left[pl.ds(l * room + base, 8), :] = a
            left[pl.ds((l + 16) * room + base, 8), :] = a * cu16 + b * su16
            right_re[pl.ds(l * room + base, 8), :] = x
            right_im[pl.ds(l * room + base, 8), :] = y
            right_re[pl.ds((l + 16) * room + base, 8), :] = x * cv16 - y * sv16
            right_im[pl.ds((l + 16) * room + base, 8), :] = y * cv16 + x * sv16
            if l < 15:
                a, b = a * cu + b * su, b * cu - a * su
                x, y = x * cv - y * sv, y * cv + x * sv
        return carry

    lax.fori_loop(0, (total + 15) // 16, lambda n, c: fetch(2 * n + 1, fetch(2 * n, c)), 0)

    def widen(i, carry):
        at = pl.ds(pl.multiple_of(i * 1024, 1024), 1024)
        gains[at, :] = raw[at, :].astype(jnp.float32)
        return carry

    for i, load in enumerate(loads):
        load.wait()
        lax.fori_loop(i * part // 1024, (i + 1) * part // 1024, widen, 0)

    def image(at):
        ku = two_u[pl.ds(at, 1), :]
        kv = two_v[pl.ds(at, 1), :]
        ls = []
        for p in range(2):
            chain = [left[pl.ds((16 * j + p) * room + at, 8, stride=2 * room), :] for j in range(2)]
            for j in range(2):
                chain.append(ku * chain[-1] - chain[-2])
            ls.extend(chain)
        sides = []
        for ref in (right_re, right_im):
            chain = [ref[pl.ds(8 * q * room + at, 8, stride=room), :] for q in range(4)]
            for q in range(4):
                chain.append(kv * chain[-2] - chain[-4])
            sides.append(jnp.concatenate(chain, 0))
        l_high, l_low = split(jnp.concatenate(ls, 0))
        re_high, re_low = split(sides[0])
        im_high, im_low = split(sides[1])
        r_high = jnp.concatenate([re_high, im_high], 0)
        r_low = jnp.concatenate([re_low, im_low], 0)
        top = dot_nt(jnp.concatenate([l_high, l_low], 0), r_high)
        both = top[:SIDE] + top[SIDE:] + dot_nt(l_high, r_low)
        half = SIDE // 2
        even, odd = both[:half], both[half:]
        re = jnp.where(low, even, pltpu.roll(odd, SIDE, 1))
        im = jnp.where(low, pltpu.roll(even, SIDE, 1), odd)
        return re, im

    def weigh(turn, carry):
        half = SIDE // 2
        images = [image(turn * UNROLL + e) for e in range(UNROLL)]
        for e in range(UNROLL):
            at = turn * UNROLL + e
            entry = listed[at]
            source, c = entry // (2 * stride), entry % stride
            tag = source * tag_width + 4 * c
            sub, first, second = tags[tag], tags[tag + 2], tags[tag + 3]
            re, im = images[e]
            pr, pi = (gains[pl.ds(first * SIDE + i, half, stride=2), :] for i in range(2))
            qr, qi = (gains[pl.ds(second * SIDE + i, half, stride=2), :] for i in range(2))
            fr = pr * qr + pi * qi
            fi = pi * qr - pr * qi
            subgrids[sub, :half, :] += re * fr - im * fi
            subgrids[sub, half:, :] += re * fi + im * fr
        return carry

    lax.fori_loop(0, (total + UNROLL - 1) // UNROLL, weigh, 0)

    batch = min(8, sub_count)

    def transform(turn, carry):
        half = SIDE // 2
        first = turn * batch
        data = []
        for e in range(batch):
            both = subgrids[first + e]
            data.append(jnp.concatenate([both[:half], both[half:]], 1))
        d_high, d_low = split(jnp.concatenate(data, 0))
        mid = dot(d_high, col_high[...]) + dot(d_low, col_high[...]) + dot(d_high, col_low[...])
        table = rows[...]
        for e in range(batch):
            part = mid[e * half : (e + 1) * half]
            stack = jnp.concatenate([part[:, q * LANES : (q + 1) * LANES] for q in range(4)], 0)
            s_high, s_low = split(stack)
            patch = dot(table, jnp.concatenate([s_high, s_high, s_low], 0))
            for k in range(pieces):
                outs[k][first + e] = patch[k * piece_rows : (k + 1) * piece_rows]
        return carry

    lax.fori_loop(0, sub_count // batch, transform, 0)


def spectrum_kernel(
    pieces, stripe_rows, tags, *refs
):
    own, below = refs[:pieces], refs[pieces : 2 * pieces]
    first0, first1, turn_c, turn_s, last, out, grid = refs[2 * pieces :]
    sub_count, piece_rows, _ = own[0].shape
    tag_width = 2 * LANES
    blocks = 2 * HALF
    tile_at, row_at = lax.axis_index("tile"), lax.axis_index("row")
    row_count = lax.axis_size("row")
    lane = lax.broadcasted_iota(jnp.int32, (1, LANES), 1)
    sign = jnp.where(lane < SIDE, -1.0, 1.0)

    @pl.when(pl.program_id(0) == 0)
    def _():
        grid[...] = jnp.zeros_like(grid)
        kappa = lax.broadcasted_iota(jnp.int32, (piece_rows, LANES), 1) % SIDE
        rho = lax.broadcasted_iota(jnp.int32, (piece_rows, LANES), 0) + piece_rows * tile_at
        above = jnp.maximum(row_at - 1, 0)

        def add(ref, base, stripe, keep_late, s):
            corner_row = tags[base + 2 * s]
            corner_col = tags[base + 2 * s + 1]
            offset = corner_row - stripe * stripe_rows
            keep = (rho >= offset) if keep_late else (rho < offset)
            piece = jnp.where(keep, ref[s], 0.0)
            block = corner_col // SIDE
            ahead = jnp.where(kappa >= corner_col % SIDE, piece, 0.0)
            here = pl.multiple_of(block * piece_rows, piece_rows)
            grid[pl.ds(here, piece_rows), :] += ahead
            there = pl.multiple_of(((block + 1) % blocks) * piece_rows, piece_rows)
            grid[pl.ds(there, piece_rows), :] += piece - ahead

        for k in range(pieces):
            source = (tile_at - k + pieces) % pieces
            for ref, stripe, keep_late in ((own[k], row_at, True), (below[k], above, False)):
                base = (source * row_count + stripe) * tag_width + LANES

                def body(s, carry, ref=ref, base=base, stripe=stripe, keep_late=keep_late):
                    add(ref, base, stripe, keep_late, s)
                    return carry

                lax.fori_loop(0, sub_count, body, 0, unroll=4)

    rows_here = out.shape[2] // (4 * SIDE)

    def pair(index, carry):
        outs = []
        for p, table in ((0, first0), (1, first1)):
            cols, turned = [], []
            for e in range(2):
                row = pl.program_id(0) * rows_here + 2 * index + e
                x = grid[pl.ds(p * piece_rows + row, HALF, stride=2 * piece_rows), :]
                cols.append(x)
                turned.append(pltpu.roll(x, SIDE, 1) * sign)
            data = jnp.concatenate([jnp.concatenate(cols, 1), jnp.concatenate(turned, 1)], 0)
            high, low = split(data)
            top = dot(table[...], high)
            outs.append(top[:HALF] + top[HALF:] + dot(table[:HALF, :], low))
        halves = (outs[0] + outs[1], outs[0] - outs[1])
        for e in range(2):
            parts = []
            for h in range(2):
                y = halves[h][:, e * LANES : (e + 1) * LANES]
                at = pl.ds(h * HALF, HALF)
                parts.append(y * turn_c[at, :] + pltpu.roll(y, SIDE, 1) * turn_s[at, :])
            high, low = split(jnp.concatenate(parts, 0))
            top = dot_nt(last[...], high)
            z = top[:LANES] + top[LANES:] + dot_nt(last[:LANES, :], low)
            for c in range(2):
                for q in range(4):
                    begin = q * rows_here + 2 * index + e
                    out[c, 0, pl.ds(begin, SIDE, stride=4 * rows_here), :] = z[
                        c * SIDE : (c + 1) * SIDE, q * LANES : (q + 1) * LANES
                    ]
        return carry

    lax.fori_loop(0, rows_here // 2, pair, 0)


def local(
    visibilities, uv_cells, block_owner, block_subgrid, block_count, block_stations, corners, aterms
):
    tile_count = lax.axis_size("tile")
    row_count = lax.axis_size("row")
    owner_count = tile_count * row_count
    blocks_here = visibilities.shape[0]
    sub_count = corners.shape[0]
    stations = aterms.shape[0]
    capacity = max(2, 3 * blocks_here // owner_count)
    stride = 8 * (-(-(capacity + 2) // 8))
    stripe_rows = SLAB // row_count
    piece_rows = stripe_rows // tile_count
    smem = pl.BlockSpec(memory_space=pltpu.SMEM)
    vmem = pl.BlockSpec(memory_space=pltpu.VMEM)

    message = pl.pallas_call(
        functools.partial(pack_kernel, capacity, stride),
        out_shape=jax.ShapeDtypeStruct((2 * owner_count * stride, LANES), jnp.float32),
        in_specs=[smem] * 5 + [vmem] * 2,
        out_specs=vmem,
        scratch_shapes=[pltpu.SMEM((owner_count,), jnp.int32)],
        name="pack",
    )(
        block_owner.reshape(-1),
        block_subgrid,
        block_count,
        block_stations.T,
        corners.T,
        visibilities,
        uv_cells,
    )
    got = lax.all_to_all(
        message.reshape(owner_count, 2, stride, LANES),
        ("tile", "row"),
        split_axis=0,
        concat_axis=0,
        tiled=True,
    )
    tags = got[:, :, capacity, :].astype(jnp.int32).reshape(-1)
    got = got.reshape(2 * owner_count * stride, LANES)

    line = aterms.shape[2] // LANES
    aterms = aterms.reshape(stations, 2, line, LANES).transpose(0, 2, 1, 3).reshape(-1, LANES)
    col_high, col_low = split_table(column_table())
    window = lax.dynamic_slice(
        jnp.asarray(row_table()), (piece_rows * lax.axis_index("tile"), 0), (SIDE, 6 * SIDE)
    )
    room = owner_count * capacity + UNROLL
    patches = pl.pallas_call(
        functools.partial(grid_kernel, capacity, stride, tile_count),
        out_shape=[
            jax.ShapeDtypeStruct((sub_count, piece_rows, LANES), jnp.float32)
            for _ in range(tile_count)
        ],
        in_specs=[smem, vmem, pl.BlockSpec(memory_space=pl.ANY)] + [vmem] * 3,
        out_specs=[vmem] * tile_count,
        scratch_shapes=[
            pltpu.VMEM((room, LANES), jnp.float32),
            pltpu.VMEM((room, LANES), jnp.float32),
            pltpu.VMEM((32 * room, LANES), jnp.float32),
            pltpu.VMEM((32 * room, LANES), jnp.float32),
            pltpu.VMEM((32 * room, LANES), jnp.float32),
            pltpu.VMEM((room, LANES), jnp.float32),
            pltpu.VMEM((room, LANES), jnp.float32),
            pltpu.VMEM((sub_count, SIDE, LANES), jnp.float32),
            pltpu.VMEM(aterms.shape, aterms.dtype),
            pltpu.VMEM(aterms.shape, jnp.float32),
            pltpu.SMEM((room + 8,), jnp.int32),
            pltpu.SemaphoreType.DMA((PARTS,)),
        ],
        compiler_params=pltpu.CompilerParams(vmem_limit_bytes=50 * 1024 * 1024),
        name="gridding",
    )(tags, got, aterms, col_high, col_low, window)

    own, below = [], []
    down = [(i, i + 1) for i in range(row_count - 1)]
    for k in range(tile_count):
        piece = patches[k]
        if k > 0:
            piece = lax.ppermute(piece, "tile", [(i, (i + k) % tile_count) for i in range(tile_count)])
        own.append(piece)
        below.append(lax.ppermute(piece, "row", down))

    first0, first1 = stage_tables()
    turn_c, turn_s = twiddle_tables()
    rows_here = min(8, piece_rows)
    steps = piece_rows // rows_here
    depth = rows_here * GRID // LANES
    spectrum = pl.pallas_call(
        functools.partial(spectrum_kernel, tile_count, stripe_rows),
        grid=(steps,),
        out_shape=jax.ShapeDtypeStruct((2, steps, depth, LANES), jnp.float32),
        in_specs=[smem] + [vmem] * (2 * tile_count + 5),
        out_specs=pl.BlockSpec((2, 1, depth, LANES), lambda i: (0, i, 0, 0)),
        scratch_shapes=[pltpu.VMEM((2 * HALF * piece_rows, LANES), jnp.float32)],
        compiler_params=pltpu.CompilerParams(vmem_limit_bytes=48 * 1024 * 1024),
        name="spectrum",
    )(tags, *own, *below, first0, first1, turn_c, turn_s, last_table())
    spectrum = spectrum.reshape(2, steps, GRID // LANES, rows_here, LANES).transpose(0, 1, 3, 2, 4)
    return spectrum.reshape(2, 1, piece_rows, GRID)


def solution(mesh):
    in_specs = (
        P(("groups", "tile", "row"), None),
        P(("groups", "tile", "row"), None),
        P(("groups", "tile", "row"), None),
        P(("groups", "tile", "row")),
        P(("groups", "tile", "row")),
        P(("groups", "tile", "row"), None),
        P(("groups", "tile", "row"), None),
        P(),
    )
    out_specs = P(None, ("groups", "row"), "tile", None)
    return jax.shard_map(local, mesh=mesh, in_specs=in_specs, out_specs=out_specs, check_vma=False)
```

```python
import functools
import math

import jax
import jax.numpy as jnp
import numpy as np
from jax import lax
from jax.experimental import pallas as pl
from jax.experimental.pallas import tpu as pltpu
from jax.sharding import PartitionSpec as P

GRID = 32768
SLAB = 256
SIDE = 64
LANES = 128
UNROLL = 16
PARTS = 8
QUARTER = GRID // SIDE // 4

SIN_TERMS = (
    6.2831852724479385, -41.3416970381994, 81.60502363801741, -76.70153767001833,
    42.01607576032372, -14.868322746301509, 3.199338837237415,
)
COS_TERMS = (
    0.9999999890590211, -19.73920449945394, 64.93911745989672, -85.45013953089433,
    60.167630950968515, -25.967599248305554, 6.528658160795414,
)


def poly(terms, z):
    total = jnp.full_like(z, terms[-1])
    for term in terms[-2::-1]:
        total = total * z + term
    return total


def cos_sin(turns):
    rest = turns - jnp.round(turns)
    z = rest * rest
    return poly(COS_TERMS, z), rest * poly(SIN_TERMS, z)


def split(x):
    high = x.astype(jnp.bfloat16)
    return high, (x - high.astype(jnp.float32)).astype(jnp.bfloat16)


def split_table(table):
    high = table.astype(jnp.bfloat16)
    return high, (table - high.astype(np.float64)).astype(jnp.bfloat16)


def dot(a, b):
    return jnp.dot(a, b, preferred_element_type=jnp.float32)


def dot_nt(a, b):
    return lax.dot_general(a, b, (((1,), (1,)), ((), ())), preferred_element_type=jnp.float32)


def taper():
    edge = (2.0 * np.arange(SIDE) + 1.0) / SIDE - 1.0
    return 1.0 - 0.9 * edge * edge


def column_table():
    m = np.arange(SIDE)
    angle = 2.0 * np.pi * (m[:, None] * m[None, :] % SIDE) / SIDE
    scale = 1.0 / (SIDE * math.sqrt(SIDE) * math.sqrt(GRID))
    real = scale * taper()[:, None] * np.cos(angle)
    imag = -scale * taper()[:, None] * np.sin(angle)
    table = np.zeros((2, 2, SIDE, 2, 2, 2, SIDE))
    for p in range(2):
        table[0, p, :, 0, p, 0] = real
        table[0, p, :, 0, p, 1] = imag
        table[1, p, :, 0, p, 0] = -imag
        table[1, p, :, 0, p, 1] = real
        table[0, p, :, 1, p, 0] = -imag
        table[0, p, :, 1, p, 1] = real
        table[1, p, :, 1, p, 0] = -real
        table[1, p, :, 1, p, 1] = -imag
    return table.reshape(4 * SIDE, 8 * SIDE)


def row_table():
    rho = np.arange(2 * SIDE) % SIDE
    a = np.arange(SIDE // 2)
    blocks = []
    for kind in (np.cos, lambda t: -np.sin(t)):
        for p in range(2):
            l = 2 * a + p
            blocks.append(taper()[l][None, :] * kind(2.0 * np.pi * (rho[:, None] * l[None, :] % SIDE) / SIDE))
    return np.concatenate(blocks, 1).astype(np.float32)


def stage_table():
    k = np.arange(QUARTER)[:, None]
    t = np.arange(QUARTER)[None, :]
    out = []
    for p in range(4):
        angle = 2.0 * np.pi * (k * (4 * t + p) % (4 * QUARTER)) / (4 * QUARTER)
        high, low = split_table(np.concatenate([np.cos(angle), -np.sin(angle)], 1))
        out.append(np.concatenate([high, low], 0))
    return np.stack(out)


def twiddle_tables():
    k = np.arange(4 * QUARTER)[:, None]
    kappa = np.arange(SIDE)[None, :]
    angle = 2.0 * np.pi * (k * kappa % GRID) / GRID
    c, s = np.cos(angle), np.sin(angle)
    return (
        np.concatenate([c, c], 1).astype(np.float32),
        np.concatenate([s, -s], 1).astype(np.float32),
    )


def last_table():
    k = np.arange(SIDE)[:, None]
    kappa = np.arange(SIDE)[None, :]
    angle = 2.0 * np.pi * (k * kappa % SIDE) / SIDE
    c, s = np.cos(angle), np.sin(angle)
    high, low = split_table(np.block([[c, s], [-s, c]]))
    return np.concatenate([high, low], 0)


def pack_kernel(capacity, stride, owner, sub, count, stations, corners, vis, uv, message, used):
    owners = message.shape[0] // (2 * stride)
    blocks = vis.shape[0]
    lane = lax.broadcasted_iota(jnp.int32, (1, LANES), 1)
    message[...] = jnp.zeros_like(message)

    def corner(i, row):
        return jnp.where(lane == i, corners[i % 2, i // 2].astype(jnp.float32), row)

    corner_row = lax.fori_loop(0, 2 * corners.shape[1], corner, jnp.zeros((1, LANES), jnp.float32), unroll=8)

    def clear(o, carry):
        used[o] = 0
        message[pl.ds((2 * o + 1) * stride + capacity, 1), :] = corner_row
        return carry

    lax.fori_loop(0, owners, clear, 0, unroll=8)

    def place(g, carry):
        o = owner[g]
        slot = used[o]
        used[o] = slot + 1
        row = 2 * o * stride + slot
        live = (lane % SIDE) < count[g]
        message[pl.ds(row, 1), :] = jnp.where(live, vis[pl.ds(g, 1), :], 0.0)
        message[pl.ds(row + stride, 1), :] = uv[pl.ds(g, 1), :]
        tags_at = pl.ds(2 * o * stride + capacity, 1)
        tag_row = message[tags_at, :]
        at = 4 * slot
        for i, value in enumerate((sub[g], count[g], stations[0, g], stations[1, g])):
            tag_row = jnp.where(lane == at + i, value.astype(jnp.float32), tag_row)
        message[tags_at, :] = tag_row
        return carry

    lax.fori_loop(0, blocks, place, 0, unroll=4)


def grid_kernel(
    capacity, stride, pieces, tags, got, aterms, col, rows, *refs
):
    outs, (rows_v, rows_uv, left, right_re, right_im, two_u, two_v, subgrids, raw, gains, col_here, rows_here, listed, arrived) = (
        refs[:pieces],
        refs[pieces:],
    )
    owners = got.shape[0] // (2 * stride)
    shift = (2 * stride).bit_length() - 1
    sub_count = outs[0].shape[0]
    piece_rows = outs[0].shape[1]
    room = rows_v.shape[0]
    lane = lax.broadcasted_iota(jnp.int32, (1, LANES), 1)
    low = lane < SIDE
    tag_width = 2 * LANES
    tile_at, row_at = lax.axis_index("tile"), lax.axis_index("row")
    mine = (tile_at * lax.axis_size("row") + row_at) * tag_width + LANES

    part = aterms.shape[0] // PARTS
    loads = [
        pltpu.make_async_copy(
            aterms.at[pl.ds(i * part, part)], raw.at[pl.ds(i * part, part)], arrived.at[i]
        )
        for i in range(PARTS)
    ]
    loads.append(pltpu.make_async_copy(col, col_here, arrived.at[PARTS]))
    loads.append(pltpu.make_async_copy(rows, rows_here, arrived.at[PARTS + 1]))
    for load in loads:
        load.start()
    subgrids[...] = jnp.zeros_like(subgrids)

    def collect(source, found):
        for c in range(capacity):
            listed[found] = 2 * source * stride + c
            found = found + (tags[source * tag_width + 4 * c + 1] > 0).astype(jnp.int32)
        return found

    total = lax.fori_loop(0, owners, collect, jnp.int32(0))
    for i in range(UNROLL):
        listed[total + i] = capacity + 1

    def fetch(n, carry):
        for e in range(8):
            at = n * 8 + e
            entry = listed[at]
            source, c = entry >> shift, entry & (stride - 1)
            sub = tags[source * tag_width + 4 * c]
            shift_u = (tags[mine + 2 * sub] & (SIDE - 1)).astype(jnp.float32)
            shift_v = (tags[mine + 2 * sub + 1] & (SIDE - 1)).astype(jnp.float32)
            rows_v[pl.ds(at, 1), :] = got[pl.ds(entry, 1), :]
            rows_uv[pl.ds(at, 1), :] = got[pl.ds(entry + stride, 1), :] + jnp.where(low, shift_u, shift_v)
        base = pl.multiple_of(n * 8, 8)
        v = rows_v[pl.ds(base, 8), :]
        turns = rows_uv[pl.ds(base, 8), :] * (1.0 / SIDE)
        c1, s1 = cos_sin(turns)
        c16, s16 = cos_sin(turns * 16.0)
        rc1, rs1 = pltpu.roll(c1, SIDE, 1), pltpu.roll(s1, SIDE, 1)
        rc16, rs16 = pltpu.roll(c16, SIDE, 1), pltpu.roll(s16, SIDE, 1)
        cu, su = jnp.where(low, c1, rc1), jnp.where(low, s1, rs1)
        cv, sv = jnp.where(low, rc1, c1), jnp.where(low, rs1, s1)
        cu16, su16 = jnp.where(low, c16, rc16), jnp.where(low, s16, rs16)
        cv16, sv16 = jnp.where(low, rc16, c16), jnp.where(low, rs16, s16)
        two_u[pl.ds(base, 8), :] = 2.0 * cu16
        two_v[pl.ds(base, 8), :] = 2.0 * cv16
        a = v
        b = pltpu.roll(v, SIDE, 1) * jnp.where(low, -1.0, 1.0)
        x = jnp.broadcast_to(jnp.where(low, 1.0, 0.0), v.shape)
        y = jnp.broadcast_to(jnp.where(low, 0.0, 1.0), v.shape)
        for l in range(16):
            left[pl.ds(l * room + base, 8), :] = a
            left[pl.ds((l + 16) * room + base, 8), :] = a * cu16 + b * su16
            right_re[pl.ds(l * room + base, 8), :] = x
            right_im[pl.ds(l * room + base, 8), :] = y
            right_re[pl.ds((l + 16) * room + base, 8), :] = x * cv16 - y * sv16
            right_im[pl.ds((l + 16) * room + base, 8), :] = y * cv16 + x * sv16
            if l < 15:
                a, b = a * cu + b * su, b * cu - a * su
                x, y = x * cv - y * sv, y * cv + x * sv
        return carry

    lax.fori_loop(0, (total + 15) // 16, lambda n, c: fetch(2 * n + 1, fetch(2 * n, c)), 0)

    def widen(i, carry):
        at = pl.ds(pl.multiple_of(i * 1024, 1024), 1024)
        gains[at, :] = raw[at, :].astype(jnp.float32)
        return carry

    for i, load in enumerate(loads[:PARTS]):
        load.wait()
        lax.fori_loop(i * part // 1024, (i + 1) * part // 1024, widen, 0)

    def image(at):
        ku = two_u[pl.ds(at, 1), :]
        kv = two_v[pl.ds(at, 1), :]
        ls = []
        for p in range(2):
            chain = [left[pl.ds((16 * j + p) * room + at, 8, stride=2 * room), :] for j in range(2)]
            for j in range(2):
                chain.append(ku * chain[-1] - chain[-2])
            ls.extend(chain)
        sides = []
        for ref in (right_re, right_im):
            chain = [ref[pl.ds(8 * q * room + at, 8, stride=room), :] for q in range(4)]
            for q in range(4):
                chain.append(kv * chain[-2] - chain[-4])
            sides.append(jnp.concatenate(chain, 0))
        l_high, l_low = split(jnp.concatenate(ls, 0))
        re_high, re_low = split(sides[0])
        im_high, im_low = split(sides[1])
        r_high = jnp.concatenate([re_high, im_high], 0)
        r_low = jnp.concatenate([re_low, im_low], 0)
        top = dot_nt(jnp.concatenate([l_high, l_low], 0), r_high)
        both = top[:SIDE] + top[SIDE:] + dot_nt(l_high, r_low)
        half = SIDE // 2
        even, odd = both[:half], both[half:]
        re = jnp.where(low, even, pltpu.roll(odd, SIDE, 1))
        im = jnp.where(low, pltpu.roll(even, SIDE, 1), odd)
        return re, im

    def weigh(turn, carry):
        half = SIDE // 2
        images = [image(turn * UNROLL + e) for e in range(UNROLL)]
        for e in range(UNROLL):
            at = turn * UNROLL + e
            entry = listed[at]
            source, c = entry >> shift, entry & (stride - 1)
            tag = source * tag_width + 4 * c
            sub, first, second = tags[tag], tags[tag + 2], tags[tag + 3]
            re, im = images[e]
            pr, pi = (gains[pl.ds(first * SIDE + i, half, stride=2), :] for i in range(2))
            qr, qi = (gains[pl.ds(second * SIDE + i, half, stride=2), :] for i in range(2))
            fr = pr * qr + pi * qi
            fi = pi * qr - pr * qi
            subgrids[sub, :half, :] += re * fr - im * fi
            subgrids[sub, half:, :] += re * fi + im * fr
        return carry

    lax.fori_loop(0, (total + UNROLL - 1) // UNROLL, weigh, 0)

    loads[PARTS].wait()
    loads[PARTS + 1].wait()
    batch = min(8, sub_count)
    table_high, table_low = split(rows_here[pl.ds(tile_at * piece_rows, SIDE), :])
    table = jnp.concatenate([table_high, table_low, table_high], 1)

    def transform(turn, carry):
        half = SIDE // 2
        first = turn * batch
        data = []
        for e in range(batch):
            both = subgrids[first + e]
            data.append(jnp.concatenate([both[:half], both[half:]], 1))
        d_high, d_low = split(jnp.concatenate(data, 0))
        mid = dot(d_high, col_here[0]) + dot(d_low, col_here[0]) + dot(d_high, col_here[1])
        for e in range(batch):
            part = mid[e * half : (e + 1) * half]
            stack = jnp.concatenate([part[:, q * LANES : (q + 1) * LANES] for q in range(4)], 0)
            s_high, s_low = split(stack)
            patch = dot(table, jnp.concatenate([s_high, s_high, s_low], 0))
            for k in range(pieces):
                outs[k][first + e] = patch[k * piece_rows : (k + 1) * piece_rows]
        return carry

    lax.fori_loop(0, sub_count // batch, transform, 0)


def turn(x):
    sign = jnp.where(lax.broadcasted_iota(jnp.int32, (1, LANES), 1) < SIDE, -1.0, 1.0)
    tiles = [x[:, i : i + LANES] for i in range(0, x.shape[1], LANES)]
    return jnp.concatenate([pltpu.roll(tile, SIDE, 1) * sign for tile in tiles], 1)


def odd_pitch(rows):
    return rows + 8 * (rows // 8 % 2 == 0)


def spectrum_kernel(pieces, stripe_rows, piece_rows, tags, *refs):
    own, below = refs[:pieces], refs[pieces : 2 * pieces]
    first, turn_c, turn_s, last, out, grid, ready, sent = refs[2 * pieces :]
    sub_count, rows, _ = own[0].shape
    tag_width = 2 * LANES
    blocks = 4 * QUARTER
    pitch = odd_pitch(4 * rows)
    steps, out_rows = out.shape[1], out.shape[3] // 4
    out_pitch = odd_pitch(4 * out_rows)
    tile_at, row_at = lax.axis_index("tile"), lax.axis_index("row")
    row_count = lax.axis_size("row")

    grid[...] = jnp.zeros_like(grid)
    kappa = lax.broadcasted_iota(jnp.int32, (rows, LANES), 1) % SIDE
    rho = lax.broadcasted_iota(jnp.int32, (rows, LANES), 0) + piece_rows * tile_at
    above = jnp.maximum(row_at - 1, 0)

    def block_at(block):
        begin = (block >> 2) * pitch + (block & 3) * rows
        return pl.ds(pl.multiple_of(begin, math.gcd(rows, 8)), rows)

    def add(ref, base, stripe, keep_late, s):
        corner_row = tags[base + 2 * s]
        corner_col = tags[base + 2 * s + 1]
        offset = corner_row - stripe * stripe_rows
        keep = (rho >= offset) if keep_late else (rho < offset)
        piece = jnp.where(keep, ref[s], 0.0)
        block = corner_col >> 6
        ahead = jnp.where(kappa >= (corner_col & (SIDE - 1)), piece, 0.0)
        grid[block_at(block), :] += ahead
        grid[block_at((block + 1) & (blocks - 1)), :] += piece - ahead

    for k in range(pieces):
        source = (tile_at - k + pieces) % pieces
        for ref, stripe, keep_late in ((own[k], row_at, True), (below[k], above, False)):
            base = (source * row_count + stripe) * tag_width + LANES

            def body(s, carry, ref=ref, base=base, stripe=stripe, keep_late=keep_late):
                add(ref, base, stripe, keep_late, s)
                return carry

            lax.fori_loop(0, sub_count, body, 0, unroll=8)

    def pair(step, index):
        x = []
        for p in range(4):
            begin = p * rows + step * out_rows + 2 * index
            cols = jnp.concatenate(
                [grid[pl.ds(begin + e, QUARTER, stride=pitch), :] for e in range(2)], 1
            )
            high, low = split(cols)
            high = jnp.concatenate([high, turn(high)], 0)
            low = jnp.concatenate([low, turn(low)], 0)
            top = dot(first[p], high)
            x.append(top[:QUARTER] + top[QUARTER:] + dot(first[p, :QUARTER, :], low))
        a, b, c, d = x[0] + x[2], x[0] - x[2], x[1] + x[3], turn(x[1] - x[3])
        quarters = (a + c, b - d, a - c, b + d)
        for e in range(2):
            parts = []
            for h in range(4):
                y = quarters[h][:, e * LANES : (e + 1) * LANES]
                at = pl.ds(h * QUARTER, QUARTER)
                parts.append(y * turn_c[at, :] + pltpu.roll(y, SIDE, 1) * turn_s[at, :])
            high, low = split(jnp.concatenate(parts, 0))
            top = dot_nt(last[...], high)
            z = top[:LANES] + top[LANES:] + dot_nt(last[:LANES, :], low)
            for c in range(2):
                for q in range(4):
                    begin = q * out_rows + 2 * index + e
                    ready[step, c, pl.ds(begin, SIDE, stride=out_pitch), :] = z[
                        c * SIDE : (c + 1) * SIDE, q * LANES : (q + 1) * LANES
                    ]

    copies = []
    for step in range(steps):
        pairs = out_rows // 2
        lax.fori_loop(
            0, pairs, lambda n, carry, step=step: (pair(step, n), carry)[1], 0, unroll=True
        )
        for c in range(2):
            source = ready.at[step, c].reshape(SIDE, out_pitch, LANES)
            copies.append(
                pltpu.make_async_copy(
                    source.at[:, pl.ds(0, 4 * out_rows), :], out.at[c, step], sent.at[step, c]
                )
            )
            copies[-1].start()
    for copy in copies:
        copy.wait()


def local(
    visibilities, uv_cells, block_owner, block_subgrid, block_count, block_stations, corners, aterms
):
    tile_count = lax.axis_size("tile")
    row_count = lax.axis_size("row")
    owner_count = tile_count * row_count
    blocks_here = visibilities.shape[0]
    sub_count = corners.shape[0]
    stations = aterms.shape[0]
    capacity = max(2, 3 * blocks_here // owner_count)
    stride = max(8, 1 << (capacity + 1).bit_length())
    stripe_rows = SLAB // row_count
    piece_rows = stripe_rows // tile_count
    smem = pl.BlockSpec(memory_space=pltpu.SMEM)
    vmem = pl.BlockSpec(memory_space=pltpu.VMEM)

    message = pl.pallas_call(
        functools.partial(pack_kernel, capacity, stride),
        out_shape=jax.ShapeDtypeStruct((2 * owner_count * stride, LANES), jnp.float32),
        in_specs=[smem] * 5 + [vmem] * 2,
        out_specs=vmem,
        scratch_shapes=[pltpu.SMEM((owner_count,), jnp.int32)],
        name="pack",
    )(
        block_owner.reshape(-1),
        block_subgrid,
        block_count,
        block_stations.T,
        corners.T,
        visibilities,
        uv_cells,
    )
    got = lax.all_to_all(
        message.reshape(owner_count, 2, stride, LANES),
        ("tile", "row"),
        split_axis=0,
        concat_axis=0,
        tiled=True,
    )
    tags = got[:, :, capacity, :].astype(jnp.int32).reshape(-1)
    got = got.reshape(2 * owner_count * stride, LANES)

    line = aterms.shape[2] // LANES
    aterms = aterms.reshape(stations, 2, line, LANES).transpose(0, 2, 1, 3).reshape(-1, LANES)
    room = owner_count * capacity + UNROLL
    anywhere = pl.BlockSpec(memory_space=pl.ANY)
    hbm = pl.BlockSpec(memory_space=pltpu.HBM)
    column, rows = (
        pltpu.with_memory_space_constraint(jnp.asarray(x), pltpu.HBM)
        for x in (np.stack(split_table(column_table())), row_table())
    )
    aterms = pltpu.with_memory_space_constraint(aterms, pltpu.HBM)
    patches = pl.pallas_call(
        functools.partial(grid_kernel, capacity, stride, tile_count),
        out_shape=[
            jax.ShapeDtypeStruct((sub_count, piece_rows, LANES), jnp.float32)
            for _ in range(tile_count)
        ],
        in_specs=[smem, vmem, hbm, hbm, hbm],
        out_specs=[vmem] * tile_count,
        scratch_shapes=[
            pltpu.VMEM((room, LANES), jnp.float32),
            pltpu.VMEM((room, LANES), jnp.float32),
            pltpu.VMEM((32 * room, LANES), jnp.float32),
            pltpu.VMEM((32 * room, LANES), jnp.float32),
            pltpu.VMEM((32 * room, LANES), jnp.float32),
            pltpu.VMEM((room, LANES), jnp.float32),
            pltpu.VMEM((room, LANES), jnp.float32),
            pltpu.VMEM((sub_count, SIDE, LANES), jnp.float32),
            pltpu.VMEM(aterms.shape, aterms.dtype),
            pltpu.VMEM(aterms.shape, jnp.float32),
            pltpu.VMEM((2, 4 * SIDE, 8 * SIDE), jnp.bfloat16),
            pltpu.VMEM((2 * SIDE, 2 * SIDE), jnp.float32),
            pltpu.SMEM((room + 8,), jnp.int32),
            pltpu.SemaphoreType.DMA((PARTS + 2,)),
        ],
        compiler_params=pltpu.CompilerParams(vmem_limit_bytes=50 * 1024 * 1024),
        name="gridding",
    )(tags, got, aterms, column, rows)

    own, below = [], []
    down = [(i, i + 1) for i in range(row_count - 1)]
    for k in range(tile_count):
        piece = patches[k]
        if k > 0:
            piece = lax.ppermute(piece, "tile", [(i, (i + k) % tile_count) for i in range(tile_count)])
        own.append(piece)
        below.append(lax.ppermute(piece, "row", down))

    turn_c, turn_s = twiddle_tables()
    out_rows = min(8, piece_rows)
    steps = piece_rows // out_rows
    spectrum = pl.pallas_call(
        functools.partial(spectrum_kernel, tile_count, stripe_rows, piece_rows),
        out_shape=jax.ShapeDtypeStruct((2, steps, SIDE, 4 * out_rows, LANES), jnp.float32),
        in_specs=[smem] + [vmem] * (2 * tile_count + 4),
        out_specs=anywhere,
        scratch_shapes=[
            pltpu.VMEM((QUARTER * odd_pitch(4 * piece_rows), LANES), jnp.float32),
            pltpu.VMEM((steps, 2, SIDE * odd_pitch(4 * out_rows), LANES), jnp.float32),
            pltpu.SemaphoreType.DMA((steps, 2)),
        ],
        compiler_params=pltpu.CompilerParams(vmem_limit_bytes=32 * 1024 * 1024),
        name="spectrum",
    )(tags, *own, *below, stage_table(), turn_c, turn_s, last_table())
    spectrum = spectrum.reshape(2, steps, GRID // LANES, out_rows, LANES).transpose(0, 1, 3, 2, 4)
    return spectrum.reshape(2, 1, piece_rows, GRID)


def solution(mesh):
    in_specs = (
        P(("groups", "tile", "row"), None),
        P(("groups", "tile", "row"), None),
        P(("groups", "tile", "row"), None),
        P(("groups", "tile", "row")),
        P(("groups", "tile", "row")),
        P(("groups", "tile", "row"), None),
        P(("groups", "tile", "row"), None),
        P(),
    )
    out_specs = P(None, ("groups", "row"), "tile", None)
    return jax.shard_map(local, mesh=mesh, in_specs=in_specs, out_specs=out_specs, check_vma=False)
```

```python
import functools
import math

import jax
import jax.numpy as jnp
import numpy as np
from jax import lax
from jax.experimental import pallas as pl
from jax.experimental.pallas import tpu as pltpu
from jax.sharding import PartitionSpec as P

GRID = 32768
SLAB = 256
SIDE = 64
LANES = 128
UNROLL = 16
QUARTER = GRID // SIDE // 4

SIN_TERMS = (
    6.2831852724479385, -41.3416970381994, 81.60502363801741, -76.70153767001833,
    42.01607576032372, -14.868322746301509, 3.199338837237415,
)
COS_TERMS = (
    0.9999999890590211, -19.73920449945394, 64.93911745989672, -85.45013953089433,
    60.167630950968515, -25.967599248305554, 6.528658160795414,
)


def poly(terms, z):
    total = jnp.full_like(z, terms[-1])
    for term in terms[-2::-1]:
        total = total * z + term
    return total


def cos_sin(turns):
    rest = turns - jnp.round(turns)
    z = rest * rest
    return poly(COS_TERMS, z), rest * poly(SIN_TERMS, z)


def split(x):
    high = x.astype(jnp.bfloat16)
    return high, (x - high.astype(jnp.float32)).astype(jnp.bfloat16)


def split_table(table):
    high = table.astype(jnp.bfloat16)
    return high, (table - high.astype(np.float64)).astype(jnp.bfloat16)


def dot(a, b):
    return jnp.dot(a, b, preferred_element_type=jnp.float32)


def dot_nt(a, b):
    return lax.dot_general(a, b, (((1,), (1,)), ((), ())), preferred_element_type=jnp.float32)


def taper():
    edge = (2.0 * np.arange(SIDE) + 1.0) / SIDE - 1.0
    return 1.0 - 0.9 * edge * edge


def column_table():
    m = np.arange(SIDE)
    angle = 2.0 * np.pi * (m[:, None] * m[None, :] % SIDE) / SIDE
    scale = 1.0 / (SIDE * math.sqrt(SIDE) * math.sqrt(GRID))
    real = scale * taper()[:, None] * np.cos(angle)
    imag = -scale * taper()[:, None] * np.sin(angle)
    table = np.zeros((2, 2, SIDE, 2, 2, 2, SIDE))
    for p in range(2):
        table[0, p, :, 0, p, 0] = real
        table[0, p, :, 0, p, 1] = imag
        table[1, p, :, 0, p, 0] = -imag
        table[1, p, :, 0, p, 1] = real
        table[0, p, :, 1, p, 0] = -imag
        table[0, p, :, 1, p, 1] = real
        table[1, p, :, 1, p, 0] = -real
        table[1, p, :, 1, p, 1] = -imag
    return table.reshape(4 * SIDE, 8 * SIDE)


def row_table():
    rho = np.arange(2 * SIDE) % SIDE
    a = np.arange(SIDE // 2)
    blocks = []
    for kind in (np.cos, lambda t: -np.sin(t)):
        for p in range(2):
            l = 2 * a + p
            blocks.append(taper()[l][None, :] * kind(2.0 * np.pi * (rho[:, None] * l[None, :] % SIDE) / SIDE))
    return np.concatenate(blocks, 1).astype(np.float32)


def stage_table():
    k = np.arange(QUARTER)[:, None]
    t = np.arange(QUARTER)[None, :]
    out = []
    for p in range(4):
        angle = 2.0 * np.pi * (k * (4 * t + p) % (4 * QUARTER)) / (4 * QUARTER)
        high, low = split_table(np.concatenate([np.cos(angle), -np.sin(angle)], 1))
        out.append(np.concatenate([high, low], 0))
    return np.stack(out)


def twiddle_tables():
    k = np.arange(4 * QUARTER)[:, None]
    kappa = np.arange(SIDE)[None, :]
    angle = 2.0 * np.pi * (k * kappa % GRID) / GRID
    c, s = np.cos(angle), np.sin(angle)
    return (
        np.concatenate([c, c], 1).astype(np.float32),
        np.concatenate([s, -s], 1).astype(np.float32),
    )


def last_table():
    k = np.arange(SIDE)[:, None]
    kappa = np.arange(SIDE)[None, :]
    angle = 2.0 * np.pi * (k * kappa % SIDE) / SIDE
    c, s = np.cos(angle), np.sin(angle)
    high, low = split_table(np.block([[c, s], [-s, c]]))
    return np.concatenate([high, low], 0)


def pack_kernel(capacity, stride, owner, sub, count, stations, corners, vis, uv, message, used):
    owners = message.shape[0] // (2 * stride)
    blocks = vis.shape[0]
    lane = lax.broadcasted_iota(jnp.int32, (1, LANES), 1)
    message[...] = jnp.zeros_like(message)

    def corner(i, row):
        for c in range(2):
            row = jnp.where(lane == 2 * i + c, corners[c, i].astype(jnp.float32), row)
        return row

    corner_row = lax.fori_loop(
        0, corners.shape[1], corner, jnp.zeros((1, LANES), jnp.float32), unroll=True
    )

    def clear(o, carry):
        used[o] = 0
        message[pl.ds((2 * o + 1) * stride + capacity, 1), :] = corner_row
        return carry

    lax.fori_loop(0, owners, clear, 0, unroll=8)

    k_at = lane & (SIDE - 1)

    def place(g, carry):
        o = owner[g]
        slot = used[o]
        used[o] = slot + 1
        row = 2 * o * stride + slot
        live = k_at < count[g]
        message[pl.ds(row, 1), :] = jnp.where(live, vis[pl.ds(g, 1), :], 0.0)
        message[pl.ds(row + stride, 1), :] = uv[pl.ds(g, 1), :]
        tags_at = pl.ds(2 * o * stride + capacity, 1)
        tag_row = message[tags_at, :]
        at = 4 * slot
        for i, value in enumerate((sub[g], count[g], stations[0, g], stations[1, g])):
            tag_row = jnp.where(lane == at + i, value.astype(jnp.float32), tag_row)
        message[tags_at, :] = tag_row
        return carry

    lax.fori_loop(0, blocks, place, 0, unroll=16)


def grid_kernel(
    capacity, stride, pieces, tags, got, aterms, col, rows, *refs
):
    outs, (rows_v, rows_uv, left, right_re, right_im, two_u, two_v, subgrids, raw, gains, col_here, rows_here, listed, arrived, gained) = (
        refs[:pieces],
        refs[pieces:],
    )
    owners = got.shape[0] // (2 * stride)
    shift = (2 * stride).bit_length() - 1
    sub_count = outs[0].shape[0]
    piece_rows = outs[0].shape[1]
    room = rows_v.shape[0]
    lane = lax.broadcasted_iota(jnp.int32, (1, LANES), 1)
    low = lane < SIDE
    tag_width = 2 * LANES
    tile_at, row_at = lax.axis_index("tile"), lax.axis_index("row")
    mine = (tile_at * lax.axis_size("row") + row_at) * tag_width + LANES

    stations = aterms.shape[0] // SIDE
    loads = [
        pltpu.make_async_copy(col, col_here, arrived.at[0]),
        pltpu.make_async_copy(rows, rows_here, arrived.at[1]),
        pltpu.make_async_copy(aterms, raw.at[pl.ds(0, stations * SIDE)], arrived.at[2]),
    ]
    for load in loads[:2]:
        load.start()
    subgrids[...] = jnp.zeros_like(subgrids)

    def collect(source, found):
        for c in range(capacity):
            listed[found] = 2 * source * stride + c
            found = found + (tags[source * tag_width + 4 * c + 1] > 0).astype(jnp.int32)
        return found

    total = lax.fori_loop(0, owners, collect, jnp.int32(0))
    for i in range(UNROLL):
        listed[total + i] = capacity + 1
    many = total > stations // 4

    @pl.when(many)
    def _():
        loads[2].start()

    def fetch_gains(group, carry):
        for e in range(UNROLL):
            at = group * UNROLL + e
            entry = listed[at]
            tag = (entry >> shift) * tag_width + 4 * (entry & (stride - 1))
            for i in range(2):
                begin = pl.multiple_of(tags[tag + 2 + i] * SIDE, SIDE)
                pltpu.make_async_copy(
                    aterms.at[pl.ds(begin, SIDE)],
                    raw.at[pl.ds(pl.multiple_of((2 * at + i) * SIDE, SIDE), SIDE)],
                    gained.at[group],
                ).start()
        return carry

    def fetch(n):
        for e in range(8):
            at = n * 8 + e
            entry = listed[at]
            source, c = entry >> shift, entry & (stride - 1)
            tag = source * tag_width + 4 * c
            sub = tags[tag]
            shift_u = (tags[mine + 2 * sub] & (SIDE - 1)).astype(jnp.float32)
            shift_v = (tags[mine + 2 * sub + 1] & (SIDE - 1)).astype(jnp.float32)
            rows_v[pl.ds(at, 1), :] = got[pl.ds(entry, 1), :]
            rows_uv[pl.ds(at, 1), :] = got[pl.ds(entry + stride, 1), :] + jnp.where(low, shift_u, shift_v)
        base = pl.multiple_of(n * 8, 8)
        v = rows_v[pl.ds(base, 8), :]
        turns = rows_uv[pl.ds(base, 8), :] * (1.0 / SIDE)
        c1, s1 = cos_sin(turns)
        c16, s16 = cos_sin(turns * 16.0)
        rc1, rs1 = pltpu.roll(c1, SIDE, 1), pltpu.roll(s1, SIDE, 1)
        rc16, rs16 = pltpu.roll(c16, SIDE, 1), pltpu.roll(s16, SIDE, 1)
        cu, su = jnp.where(low, c1, rc1), jnp.where(low, s1, rs1)
        cv, sv = jnp.where(low, rc1, c1), jnp.where(low, rs1, s1)
        cu16, su16 = jnp.where(low, c16, rc16), jnp.where(low, s16, rs16)
        cv16, sv16 = jnp.where(low, rc16, c16), jnp.where(low, rs16, s16)
        two_u[pl.ds(base, 8), :] = 2.0 * cu16
        two_v[pl.ds(base, 8), :] = 2.0 * cv16
        a = v
        b = pltpu.roll(v, SIDE, 1) * jnp.where(low, -1.0, 1.0)
        x = jnp.broadcast_to(jnp.where(low, 1.0, 0.0), v.shape)
        y = jnp.broadcast_to(jnp.where(low, 0.0, 1.0), v.shape)
        for l in range(16):
            left[pl.ds(l * room + base, 8), :] = a
            left[pl.ds((l + 16) * room + base, 8), :] = a * cu16 + b * su16
            right_re[pl.ds(l * room + base, 8), :] = x
            right_im[pl.ds(l * room + base, 8), :] = y
            right_re[pl.ds((l + 16) * room + base, 8), :] = x * cv16 - y * sv16
            right_im[pl.ds((l + 16) * room + base, 8), :] = y * cv16 + x * sv16
            if l < 15:
                a, b = a * cu + b * su, b * cu - a * su
                x, y = x * cv - y * sv, y * cv + x * sv
    groups = (total + UNROLL - 1) // UNROLL

    def fetch_group(group, carry):
        for i in range(UNROLL // 8):
            fetch(group * (UNROLL // 8) + i)
        return carry

    lax.fori_loop(0, jnp.where(many, 0, groups), fetch_gains, 0)
    lax.fori_loop(0, groups, fetch_group, 0)

    @pl.when(many)
    def _():
        loads[2].wait()

    def image(at):
        ku = two_u[pl.ds(at, 1), :]
        kv = two_v[pl.ds(at, 1), :]
        ls = []
        for p in range(2):
            chain = [left[pl.ds((16 * j + p) * room + at, 8, stride=2 * room), :] for j in range(2)]
            for j in range(2):
                chain.append(ku * chain[-1] - chain[-2])
            ls.extend(chain)
        sides = []
        for ref in (right_re, right_im):
            chain = [ref[pl.ds(8 * q * room + at, 8, stride=room), :] for q in range(4)]
            for q in range(4):
                chain.append(kv * chain[-2] - chain[-4])
            sides.append(jnp.concatenate(chain, 0))
        l_high, l_low = split(jnp.concatenate(ls, 0))
        re_high, re_low = split(sides[0])
        im_high, im_low = split(sides[1])
        r_high = jnp.concatenate([re_high, im_high], 0)
        r_low = jnp.concatenate([re_low, im_low], 0)
        top = dot_nt(jnp.concatenate([l_high, l_low], 0), r_high)
        both = top[:SIDE] + top[SIDE:] + dot_nt(l_high, r_low)
        half = SIDE // 2
        even, odd = both[:half], both[half:]
        re = jnp.where(low, even, pltpu.roll(odd, SIDE, 1))
        im = jnp.where(low, pltpu.roll(even, SIDE, 1), odd)
        return re, im

    span = 2 * UNROLL * SIDE

    def weigh(turn, carry):
        half = SIDE // 2
        begin = pl.multiple_of(turn * span, span)

        @pl.when(jnp.logical_not(many))
        def _():
            pltpu.make_async_copy(
                aterms.at[pl.ds(0, span)], raw.at[pl.ds(begin, span)], gained.at[turn]
            ).wait()

        for e in range(UNROLL):
            at = turn * UNROLL + e
            entry = listed[at]
            tag = (entry >> shift) * tag_width + 4 * (entry & (stride - 1))
            for i in range(2):
                row = pl.multiple_of(
                    jnp.where(many, tags[tag + 2 + i] * SIDE, (2 * at + i) * SIDE), SIDE
                )
                gains[(2 * e + i) * SIDE : (2 * e + i + 1) * SIDE, :] = raw[
                    pl.ds(row, SIDE), :
                ].astype(jnp.float32)
        images = [image(turn * UNROLL + e) for e in range(UNROLL)]
        for e in range(UNROLL):
            at = turn * UNROLL + e
            entry = listed[at]
            source, c = entry >> shift, entry & (stride - 1)
            tag = source * tag_width + 4 * c
            sub = tags[tag]
            re, im = images[e]
            pr, pi = (gains[pl.ds(2 * e * SIDE + i, half, stride=2), :] for i in range(2))
            qr, qi = (gains[pl.ds((2 * e + 1) * SIDE + i, half, stride=2), :] for i in range(2))
            fr = pr * qr + pi * qi
            fi = pi * qr - pr * qi
            subgrids[sub, :half, :] += re * fr - im * fi
            subgrids[sub, half:, :] += re * fi + im * fr
        return carry

    lax.fori_loop(0, groups, weigh, 0)

    loads[0].wait()
    loads[1].wait()
    batch = min(8, sub_count)
    table_high, table_low = split(rows_here[pl.ds(tile_at * piece_rows, SIDE), :])
    table = jnp.concatenate([table_high, table_low], 0)

    def transform(turn, carry):
        half = SIDE // 2
        first = turn * batch
        data = []
        for e in range(batch):
            both = subgrids[first + e]
            data.append(jnp.concatenate([both[:half], both[half:]], 1))
        d_high, d_low = split(jnp.concatenate(data, 0))
        mid = dot(d_high, col_here[0]) + dot(d_low, col_here[0]) + dot(d_high, col_here[1])
        for e in range(0, batch, 2):
            stack = []
            for part in (mid[e * half : (e + 1) * half], mid[(e + 1) * half : (e + 2) * half]):
                stack.append(jnp.concatenate([part[:, q * LANES : (q + 1) * LANES] for q in range(4)], 0))
            s_high, s_low = split(jnp.concatenate(stack, 1))
            top = dot(table, s_high)
            patch = top[:SIDE] + top[SIDE:] + dot(table_high, s_low)
            for k in range(pieces):
                for i in range(2):
                    outs[k][first + e + i] = patch[k * piece_rows : (k + 1) * piece_rows, i * LANES : (i + 1) * LANES]
        return carry

    lax.fori_loop(0, sub_count // batch, transform, 0, unroll=2)


def turn(x):
    sign = jnp.where(lax.broadcasted_iota(jnp.int32, (1, LANES), 1) < SIDE, -1.0, 1.0)
    tiles = [x[:, i : i + LANES] for i in range(0, x.shape[1], LANES)]
    return jnp.concatenate([pltpu.roll(tile, SIDE, 1) * sign for tile in tiles], 1)


def odd_pitch(rows):
    return rows + 8 * (rows // 8 % 2 == 0)


def spectrum_kernel(pieces, stripe_rows, piece_rows, tags, *refs):
    own, below = refs[:pieces], refs[pieces : 2 * pieces]
    first, turn_c, turn_s, last, out, grid, ready, sent = refs[2 * pieces :]
    sub_count, rows, _ = own[0].shape
    tag_width = 2 * LANES
    blocks = 4 * QUARTER
    pitch = odd_pitch(4 * rows)
    steps, out_rows = out.shape[1], out.shape[3] // 4
    out_pitch = odd_pitch(4 * out_rows)
    tile_at, row_at = lax.axis_index("tile"), lax.axis_index("row")
    row_count = lax.axis_size("row")

    grid[...] = jnp.zeros_like(grid)
    kappa = lax.broadcasted_iota(jnp.int32, (rows, LANES), 1) % SIDE
    rho = lax.broadcasted_iota(jnp.int32, (rows, LANES), 0) + piece_rows * tile_at
    above = jnp.maximum(row_at - 1, 0)

    def block_at(block):
        begin = (block >> 2) * pitch + (block & 3) * rows
        return pl.ds(pl.multiple_of(begin, math.gcd(rows, 8)), rows)

    def add(ref, base, stripe, keep_late, s):
        corner_row = tags[base + 2 * s]
        corner_col = tags[base + 2 * s + 1]
        offset = corner_row - stripe * stripe_rows
        keep = (rho >= offset) if keep_late else (rho < offset)
        piece = jnp.where(keep, ref[s], 0.0)
        block = corner_col >> 6
        ahead = jnp.where(kappa >= (corner_col & (SIDE - 1)), piece, 0.0)
        grid[block_at(block), :] += ahead
        grid[block_at((block + 1) & (blocks - 1)), :] += piece - ahead

    for k in range(pieces):
        source = (tile_at - k + pieces) % pieces
        for ref, stripe, keep_late in ((own[k], row_at, True), (below[k], above, False)):
            base = (source * row_count + stripe) * tag_width + LANES

            def body(s, carry, ref=ref, base=base, stripe=stripe, keep_late=keep_late):
                add(ref, base, stripe, keep_late, s)
                return carry

            lax.fori_loop(0, sub_count, body, 0, unroll=8)

    def pair(step, index):
        x = []
        for p in range(4):
            begin = p * rows + step * out_rows + 2 * index
            cols = jnp.concatenate(
                [grid[pl.ds(begin + e, QUARTER, stride=pitch), :] for e in range(2)], 1
            )
            high, low = split(cols)
            high = jnp.concatenate([high, turn(high)], 0)
            low = jnp.concatenate([low, turn(low)], 0)
            top = dot(first[p], high)
            x.append(top[:QUARTER] + top[QUARTER:] + dot(first[p, :QUARTER, :], low))
        a, b, c, d = x[0] + x[2], x[0] - x[2], x[1] + x[3], turn(x[1] - x[3])
        quarters = (a + c, b - d, a - c, b + d)
        for e in range(2):
            parts = []
            for h in range(4):
                y = quarters[h][:, e * LANES : (e + 1) * LANES]
                at = pl.ds(h * QUARTER, QUARTER)
                parts.append(y * turn_c[at, :] + pltpu.roll(y, SIDE, 1) * turn_s[at, :])
            high, low = split(jnp.concatenate(parts, 0))
            top = dot_nt(last[...], high)
            z = top[:LANES] + top[LANES:] + dot_nt(last[:LANES, :], low)
            for c in range(2):
                for q in range(4):
                    begin = q * out_rows + 2 * index + e
                    ready[step, c, pl.ds(begin, SIDE, stride=out_pitch), :] = z[
                        c * SIDE : (c + 1) * SIDE, q * LANES : (q + 1) * LANES
                    ]

    copies = []
    for step in range(steps):
        pairs = out_rows // 2
        lax.fori_loop(
            0, pairs, lambda n, carry, step=step: (pair(step, n), carry)[1], 0, unroll=True
        )
        for c in range(2):
            source = ready.at[step, c].reshape(SIDE, out_pitch, LANES)
            copies.append(
                pltpu.make_async_copy(
                    source.at[:, pl.ds(0, 4 * out_rows), :], out.at[c, step], sent.at[step, c]
                )
            )
            copies[-1].start()
    for copy in copies:
        copy.wait()


def local(
    visibilities, uv_cells, block_owner, block_subgrid, block_count, block_stations, corners, aterms
):
    tile_count = lax.axis_size("tile")
    row_count = lax.axis_size("row")
    owner_count = tile_count * row_count
    blocks_here = visibilities.shape[0]
    sub_count = corners.shape[0]
    stations = aterms.shape[0]
    capacity = max(2, 3 * blocks_here // owner_count)
    stride = max(8, 1 << (capacity + 1).bit_length())
    stripe_rows = SLAB // row_count
    piece_rows = stripe_rows // tile_count
    smem = pl.BlockSpec(memory_space=pltpu.SMEM)
    vmem = pl.BlockSpec(memory_space=pltpu.VMEM)

    message = pl.pallas_call(
        functools.partial(pack_kernel, capacity, stride),
        out_shape=jax.ShapeDtypeStruct((2 * owner_count * stride, LANES), jnp.float32),
        in_specs=[smem] * 5 + [vmem] * 2,
        out_specs=vmem,
        scratch_shapes=[pltpu.SMEM((owner_count,), jnp.int32)],
        name="pack",
    )(
        block_owner.reshape(-1),
        block_subgrid,
        block_count,
        block_stations.T,
        corners.T,
        visibilities,
        uv_cells,
    )
    got = lax.all_to_all(
        message.reshape(owner_count, 2, stride, LANES),
        ("tile", "row"),
        split_axis=0,
        concat_axis=0,
        tiled=True,
    )
    tags = got[:, :, capacity, :].astype(jnp.int32).reshape(-1)
    got = got.reshape(2 * owner_count * stride, LANES)

    line = aterms.shape[2] // LANES
    aterms = aterms.reshape(stations, 2, line, LANES).transpose(0, 2, 1, 3).reshape(-1, LANES)
    room = UNROLL * (owner_count * capacity // UNROLL + 1)
    anywhere = pl.BlockSpec(memory_space=pl.ANY)
    hbm = pl.BlockSpec(memory_space=pltpu.HBM)
    column, rows = (
        pltpu.with_memory_space_constraint(jnp.asarray(x), pltpu.HBM)
        for x in (np.stack(split_table(column_table())), row_table())
    )
    aterms = pltpu.with_memory_space_constraint(aterms, pltpu.HBM)
    patches = pl.pallas_call(
        functools.partial(grid_kernel, capacity, stride, tile_count),
        out_shape=[
            jax.ShapeDtypeStruct((sub_count, piece_rows, LANES), jnp.float32)
            for _ in range(tile_count)
        ],
        in_specs=[smem, vmem, hbm, hbm, hbm],
        out_specs=[vmem] * tile_count,
        scratch_shapes=[
            pltpu.VMEM((room, LANES), jnp.float32),
            pltpu.VMEM((room, LANES), jnp.float32),
            pltpu.VMEM((32 * room, LANES), jnp.float32),
            pltpu.VMEM((32 * room, LANES), jnp.float32),
            pltpu.VMEM((32 * room, LANES), jnp.float32),
            pltpu.VMEM((room, LANES), jnp.float32),
            pltpu.VMEM((room, LANES), jnp.float32),
            pltpu.VMEM((sub_count, SIDE, LANES), jnp.float32),
            pltpu.VMEM((max(2 * room, stations) * SIDE, LANES), aterms.dtype),
            pltpu.VMEM((2 * UNROLL * SIDE, LANES), jnp.float32),
            pltpu.VMEM((2, 4 * SIDE, 8 * SIDE), jnp.bfloat16),
            pltpu.VMEM((2 * SIDE, 2 * SIDE), jnp.float32),
            pltpu.SMEM((room + 8,), jnp.int32),
            pltpu.SemaphoreType.DMA((3,)),
            pltpu.SemaphoreType.DMA((room // UNROLL,)),
        ],
        compiler_params=pltpu.CompilerParams(vmem_limit_bytes=50 * 1024 * 1024),
        name="gridding",
    )(tags, got, aterms, column, rows)

    own, below = [], []
    down = [(i, i + 1) for i in range(row_count - 1)]
    for k in range(tile_count):
        piece = patches[k]
        if k > 0:
            piece = lax.ppermute(piece, "tile", [(i, (i + k) % tile_count) for i in range(tile_count)])
        own.append(piece)
        below.append(lax.ppermute(piece, "row", down))

    turn_c, turn_s = twiddle_tables()
    out_rows = min(8, piece_rows)
    steps = piece_rows // out_rows
    spectrum = pl.pallas_call(
        functools.partial(spectrum_kernel, tile_count, stripe_rows, piece_rows),
        out_shape=jax.ShapeDtypeStruct((2, steps, SIDE, 4 * out_rows, LANES), jnp.float32),
        in_specs=[smem] + [vmem] * (2 * tile_count + 4),
        out_specs=anywhere,
        scratch_shapes=[
            pltpu.VMEM((QUARTER * odd_pitch(4 * piece_rows), LANES), jnp.float32),
            pltpu.VMEM((steps, 2, SIDE * odd_pitch(4 * out_rows), LANES), jnp.float32),
            pltpu.SemaphoreType.DMA((steps, 2)),
        ],
        compiler_params=pltpu.CompilerParams(vmem_limit_bytes=32 * 1024 * 1024),
        name="spectrum",
    )(tags, *own, *below, stage_table(), turn_c, turn_s, last_table())
    spectrum = spectrum.reshape(2, steps, GRID // LANES, out_rows, LANES).transpose(0, 1, 3, 2, 4)
    return spectrum.reshape(2, 1, piece_rows, GRID)


def solution(mesh):
    in_specs = (
        P(("groups", "tile", "row"), None),
        P(("groups", "tile", "row"), None),
        P(("groups", "tile", "row"), None),
        P(("groups", "tile", "row")),
        P(("groups", "tile", "row")),
        P(("groups", "tile", "row"), None),
        P(("groups", "tile", "row"), None),
        P(),
    )
    out_specs = P(None, ("groups", "row"), "tile", None)
    return jax.shard_map(local, mesh=mesh, in_specs=in_specs, out_specs=out_specs, check_vma=False)
```

```python
import functools
import math

import jax
import jax.numpy as jnp
import numpy as np
from jax import lax
from jax.experimental import pallas as pl
from jax.experimental.pallas import tpu as pltpu
from jax.sharding import PartitionSpec as P

GRID = 32768
SLAB = 256
SIDE = 64
LANES = 128
UNROLL = 16
QUARTER = GRID // SIDE // 4

SIN_TERMS = (
    6.2831852724479385, -41.3416970381994, 81.60502363801741, -76.70153767001833,
    42.01607576032372, -14.868322746301509, 3.199338837237415,
)
COS_TERMS = (
    0.9999999890590211, -19.73920449945394, 64.93911745989672, -85.45013953089433,
    60.167630950968515, -25.967599248305554, 6.528658160795414,
)


def poly(terms, z):
    total = jnp.full_like(z, terms[-1])
    for term in terms[-2::-1]:
        total = total * z + term
    return total


def cos_sin(turns):
    rest = turns - jnp.round(turns)
    z = rest * rest
    return poly(COS_TERMS, z), rest * poly(SIN_TERMS, z)


def split(x):
    high = x.astype(jnp.bfloat16)
    return high, (x - high.astype(jnp.float32)).astype(jnp.bfloat16)


def split_table(table):
    high = table.astype(jnp.bfloat16)
    return high, (table - high.astype(np.float64)).astype(jnp.bfloat16)


def dot(a, b):
    return jnp.dot(a, b, preferred_element_type=jnp.float32)


def dot_nt(a, b):
    return lax.dot_general(a, b, (((1,), (1,)), ((), ())), preferred_element_type=jnp.float32)


def taper():
    edge = (2.0 * np.arange(SIDE) + 1.0) / SIDE - 1.0
    return 1.0 - 0.9 * edge * edge


def column_table():
    m = np.arange(SIDE)
    angle = 2.0 * np.pi * (m[:, None] * m[None, :] % SIDE) / SIDE
    scale = 1.0 / (SIDE * math.sqrt(SIDE) * math.sqrt(GRID))
    real = scale * taper()[:, None] * np.cos(angle)
    imag = -scale * taper()[:, None] * np.sin(angle)
    table = np.zeros((2, 2, SIDE, 2, 2, 2, SIDE))
    for p in range(2):
        table[0, p, :, 0, p, 0] = real
        table[0, p, :, 0, p, 1] = imag
        table[1, p, :, 0, p, 0] = -imag
        table[1, p, :, 0, p, 1] = real
        table[0, p, :, 1, p, 0] = -imag
        table[0, p, :, 1, p, 1] = real
        table[1, p, :, 1, p, 0] = -real
        table[1, p, :, 1, p, 1] = -imag
    return table.reshape(4 * SIDE, 8 * SIDE)


def row_table():
    rho = np.arange(2 * SIDE) % SIDE
    a = np.arange(SIDE // 2)
    blocks = []
    for kind in (np.cos, lambda t: -np.sin(t)):
        for p in range(2):
            l = 2 * a + p
            blocks.append(taper()[l][None, :] * kind(2.0 * np.pi * (rho[:, None] * l[None, :] % SIDE) / SIDE))
    return np.concatenate(blocks, 1).astype(np.float32)


def stage_table():
    k = np.arange(QUARTER)[:, None]
    t = np.arange(QUARTER)[None, :]
    out = []
    for p in range(4):
        angle = 2.0 * np.pi * (k * (4 * t + p) % (4 * QUARTER)) / (4 * QUARTER)
        high, low = split_table(np.concatenate([np.cos(angle), -np.sin(angle)], 1))
        out.append(np.concatenate([high, low], 0))
    return np.stack(out)


def twiddle_tables():
    k = np.arange(4 * QUARTER)[:, None]
    kappa = np.arange(SIDE)[None, :]
    angle = 2.0 * np.pi * (k * kappa % GRID) / GRID
    c, s = np.cos(angle), np.sin(angle)
    return (
        np.concatenate([c, c], 1).astype(np.float32),
        np.concatenate([s, -s], 1).astype(np.float32),
    )


def last_table():
    k = np.arange(SIDE)[:, None]
    kappa = np.arange(SIDE)[None, :]
    angle = 2.0 * np.pi * (k * kappa % SIDE) / SIDE
    c, s = np.cos(angle), np.sin(angle)
    high, low = split_table(np.block([[c, s], [-s, c]]))
    return np.concatenate([high, low], 0)


def pack_kernel(capacity, stride, owner, sub, count, stations, corners, vis, uv, message, used):
    owners = message.shape[0] // (2 * stride)
    blocks = vis.shape[0]
    lane = lax.broadcasted_iota(jnp.int32, (1, LANES), 1)
    message[...] = jnp.zeros_like(message)

    def corner(i, row):
        for c in range(2):
            row = jnp.where(lane == 2 * i + c, corners[c, i].astype(jnp.float32), row)
        return row

    corner_row = lax.fori_loop(
        0, corners.shape[1], corner, jnp.zeros((1, LANES), jnp.float32), unroll=True
    )

    def clear(o, carry):
        used[o] = 0
        message[pl.ds((2 * o + 1) * stride + capacity, 1), :] = corner_row
        return carry

    lax.fori_loop(0, owners, clear, 0, unroll=8)

    k_at = lane & (SIDE - 1)

    def place(g, carry):
        o = owner[g]
        slot = used[o]
        used[o] = slot + 1
        row = 2 * o * stride + slot
        live = k_at < count[g]
        message[pl.ds(row, 1), :] = jnp.where(live, vis[pl.ds(g, 1), :], 0.0)
        message[pl.ds(row + stride, 1), :] = uv[pl.ds(g, 1), :]
        tags_at = pl.ds(2 * o * stride + capacity, 1)
        tag_row = message[tags_at, :]
        at = 4 * slot
        for i, value in enumerate((sub[g], count[g], stations[0, g], stations[1, g])):
            tag_row = jnp.where(lane == at + i, value.astype(jnp.float32), tag_row)
        message[tags_at, :] = tag_row
        return carry

    lax.fori_loop(0, blocks, place, 0, unroll=16)


def grid_kernel(
    capacity, stride, pieces, tags, got, aterms, col, rows, *refs
):
    outs, (rows_v, rows_uv, left, right_re, right_im, two_u, two_v, subgrids, raw, gains, col_here, rows_here, listed, arrived, gained) = (
        refs[:pieces],
        refs[pieces:],
    )
    owners = got.shape[0] // (2 * stride)
    shift = (2 * stride).bit_length() - 1
    sub_count = outs[0].shape[0]
    piece_rows = outs[0].shape[1]
    room = rows_v.shape[0]
    lane = lax.broadcasted_iota(jnp.int32, (1, LANES), 1)
    low = lane < SIDE
    tag_width = 2 * LANES
    tile_at, row_at = lax.axis_index("tile"), lax.axis_index("row")
    mine = (tile_at * lax.axis_size("row") + row_at) * tag_width + LANES

    stations = aterms.shape[0] // SIDE
    loads = [
        pltpu.make_async_copy(col, col_here, arrived.at[0]),
        pltpu.make_async_copy(rows, rows_here, arrived.at[1]),
        pltpu.make_async_copy(aterms, raw.at[pl.ds(0, stations * SIDE)], arrived.at[2]),
    ]
    for load in loads[:2]:
        load.start()
    subgrids[...] = jnp.zeros_like(subgrids)

    def collect(source, found):
        for c in range(capacity):
            listed[found] = 2 * source * stride + c
            found = found + (tags[source * tag_width + 4 * c + 1] > 0).astype(jnp.int32)
        return found

    total = lax.fori_loop(0, owners, collect, jnp.int32(0))
    for i in range(UNROLL):
        listed[total + i] = capacity + 1
    many = total > stations // 4

    @pl.when(many)
    def _():
        loads[2].start()

    def fetch_gains(group, carry):
        for e in range(UNROLL):
            at = group * UNROLL + e
            entry = listed[at]
            tag = (entry >> shift) * tag_width + 4 * (entry & (stride - 1))
            for i in range(2):
                begin = pl.multiple_of(tags[tag + 2 + i] * SIDE, SIDE)
                pltpu.make_async_copy(
                    aterms.at[pl.ds(begin, SIDE)],
                    raw.at[pl.ds(pl.multiple_of((2 * at + i) * SIDE, SIDE), SIDE)],
                    gained.at[group],
                ).start()
        return carry

    def fetch(n):
        for e in range(8):
            at = n * 8 + e
            entry = listed[at]
            source, c = entry >> shift, entry & (stride - 1)
            tag = source * tag_width + 4 * c
            sub = tags[tag]
            shift_u = (tags[mine + 2 * sub] & (SIDE - 1)).astype(jnp.float32)
            shift_v = (tags[mine + 2 * sub + 1] & (SIDE - 1)).astype(jnp.float32)
            rows_v[pl.ds(at, 1), :] = got[pl.ds(entry, 1), :]
            rows_uv[pl.ds(at, 1), :] = got[pl.ds(entry + stride, 1), :] + jnp.where(low, shift_u, shift_v)
        base = pl.multiple_of(n * 8, 8)
        v = rows_v[pl.ds(base, 8), :]
        turns = rows_uv[pl.ds(base, 8), :] * (1.0 / SIDE)
        c1, s1 = cos_sin(turns)
        c16, s16 = cos_sin(turns * 16.0)
        rc1, rs1 = pltpu.roll(c1, SIDE, 1), pltpu.roll(s1, SIDE, 1)
        rc16, rs16 = pltpu.roll(c16, SIDE, 1), pltpu.roll(s16, SIDE, 1)
        cu, su = jnp.where(low, c1, rc1), jnp.where(low, s1, rs1)
        cv, sv = jnp.where(low, rc1, c1), jnp.where(low, rs1, s1)
        cu16, su16 = jnp.where(low, c16, rc16), jnp.where(low, s16, rs16)
        cv16, sv16 = jnp.where(low, rc16, c16), jnp.where(low, rs16, s16)
        two_u[pl.ds(base, 8), :] = 2.0 * cu16
        two_v[pl.ds(base, 8), :] = 2.0 * cv16
        a = v
        b = pltpu.roll(v, SIDE, 1) * jnp.where(low, -1.0, 1.0)
        x = jnp.broadcast_to(jnp.where(low, 1.0, 0.0), v.shape)
        y = jnp.broadcast_to(jnp.where(low, 0.0, 1.0), v.shape)
        for l in range(16):
            left[pl.ds(l * room + base, 8), :] = a
            left[pl.ds((l + 16) * room + base, 8), :] = a * cu16 + b * su16
            right_re[pl.ds(l * room + base, 8), :] = x
            right_im[pl.ds(l * room + base, 8), :] = y
            right_re[pl.ds((l + 16) * room + base, 8), :] = x * cv16 - y * sv16
            right_im[pl.ds((l + 16) * room + base, 8), :] = y * cv16 + x * sv16
            if l < 15:
                a, b = a * cu + b * su, b * cu - a * su
                x, y = x * cv - y * sv, y * cv + x * sv
    groups = (total + UNROLL - 1) // UNROLL

    def fetch_group(group, carry):
        for i in range(UNROLL // 8):
            fetch(group * (UNROLL // 8) + i)
        return carry

    lax.fori_loop(0, jnp.where(many, 0, groups), fetch_gains, 0)
    lax.fori_loop(0, groups, fetch_group, 0)

    @pl.when(many)
    def _():
        loads[2].wait()

    def image(at):
        ku = two_u[pl.ds(at, 1), :]
        kv = two_v[pl.ds(at, 1), :]
        ls = []
        for p in range(2):
            chain = [left[pl.ds((16 * j + p) * room + at, 8, stride=2 * room), :] for j in range(2)]
            for j in range(2):
                chain.append(ku * chain[-1] - chain[-2])
            ls.extend(chain)
        sides = []
        for ref in (right_re, right_im):
            chain = [ref[pl.ds(8 * q * room + at, 8, stride=room), :] for q in range(4)]
            for q in range(4):
                chain.append(kv * chain[-2] - chain[-4])
            sides.append(jnp.concatenate(chain, 0))
        l_high, l_low = split(jnp.concatenate(ls, 0))
        re_high, re_low = split(sides[0])
        im_high, im_low = split(sides[1])
        r_high = jnp.concatenate([re_high, im_high], 0)
        r_low = jnp.concatenate([re_low, im_low], 0)
        top = dot_nt(jnp.concatenate([l_high, l_low], 0), r_high)
        both = top[:SIDE] + top[SIDE:] + dot_nt(l_high, r_low)
        half = SIDE // 2
        even, odd = both[:half], both[half:]
        re = jnp.where(low, even, pltpu.roll(odd, SIDE, 1))
        im = jnp.where(low, pltpu.roll(even, SIDE, 1), odd)
        return re, im

    span = 2 * UNROLL * SIDE

    def weigh(turn, carry):
        half = SIDE // 2
        begin = pl.multiple_of(turn * span, span)

        @pl.when(jnp.logical_not(many))
        def _():
            pltpu.make_async_copy(
                aterms.at[pl.ds(0, span)], raw.at[pl.ds(begin, span)], gained.at[turn]
            ).wait()

        for e in range(UNROLL):
            at = turn * UNROLL + e
            entry = listed[at]
            tag = (entry >> shift) * tag_width + 4 * (entry & (stride - 1))
            for i in range(2):
                row = pl.multiple_of(
                    jnp.where(many, tags[tag + 2 + i] * SIDE, (2 * at + i) * SIDE), SIDE
                )
                gains[(2 * e + i) * SIDE : (2 * e + i + 1) * SIDE, :] = raw[
                    pl.ds(row, SIDE), :
                ].astype(jnp.float32)
        images = [image(turn * UNROLL + e) for e in range(UNROLL)]
        for e in range(UNROLL):
            at = turn * UNROLL + e
            entry = listed[at]
            source, c = entry >> shift, entry & (stride - 1)
            tag = source * tag_width + 4 * c
            sub = tags[tag]
            re, im = images[e]
            pr, pi = (gains[pl.ds(2 * e * SIDE + i, half, stride=2), :] for i in range(2))
            qr, qi = (gains[pl.ds((2 * e + 1) * SIDE + i, half, stride=2), :] for i in range(2))
            fr = pr * qr + pi * qi
            fi = pi * qr - pr * qi
            subgrids[sub, :half, :] += re * fr - im * fi
            subgrids[sub, half:, :] += re * fi + im * fr
        return carry

    lax.fori_loop(0, groups, weigh, 0)

    loads[0].wait()
    loads[1].wait()
    batch = min(8, sub_count)
    table_high, table_low = split(rows_here[pl.ds(tile_at * piece_rows, SIDE), :])
    table = jnp.concatenate([table_high, table_low], 0)

    def transform(turn, carry):
        half = SIDE // 2
        first = turn * batch
        data = []
        for e in range(batch):
            both = subgrids[first + e]
            data.append(jnp.concatenate([both[:half], both[half:]], 1))
        d_high, d_low = split(jnp.concatenate(data, 0))
        mid = dot(d_high, col_here[0]) + dot(d_low, col_here[0]) + dot(d_high, col_here[1])
        for e in range(0, batch, 2):
            stack = []
            for part in (mid[e * half : (e + 1) * half], mid[(e + 1) * half : (e + 2) * half]):
                stack.append(jnp.concatenate([part[:, q * LANES : (q + 1) * LANES] for q in range(4)], 0))
            s_high, s_low = split(jnp.concatenate(stack, 1))
            top = dot(table, s_high)
            patch = top[:SIDE] + top[SIDE:] + dot(table_high, s_low)
            for k in range(pieces):
                for i in range(2):
                    outs[k][first + e + i] = patch[k * piece_rows : (k + 1) * piece_rows, i * LANES : (i + 1) * LANES]
        return carry

    lax.fori_loop(0, sub_count // batch, transform, 0, unroll=2)


def turn(x):
    sign = jnp.where(lax.broadcasted_iota(jnp.int32, (1, LANES), 1) < SIDE, -1.0, 1.0)
    tiles = [x[:, i : i + LANES] for i in range(0, x.shape[1], LANES)]
    return jnp.concatenate([pltpu.roll(tile, SIDE, 1) * sign for tile in tiles], 1)


def odd_pitch(rows):
    return rows + 8 * (rows // 8 % 2 == 0)


def place(pieces, stripe_rows, stripe, keep_late, tags, grid):
    sub_count, rows, _ = pieces[0].shape
    tag_width = 2 * LANES
    blocks = 4 * QUARTER
    pitch = odd_pitch(4 * rows)
    tile_at = lax.axis_index("tile")
    row_count = lax.axis_size("row")
    kappa = lax.broadcasted_iota(jnp.int32, (rows, LANES), 1) % SIDE
    rho = lax.broadcasted_iota(jnp.int32, (rows, LANES), 0) + rows * tile_at

    def block_at(block):
        begin = (block >> 2) * pitch + (block & 3) * rows
        return pl.ds(pl.multiple_of(begin, math.gcd(rows, 8)), rows)

    for k, ref in enumerate(pieces):
        source = (tile_at - k + len(pieces)) % len(pieces)
        base = (source * row_count + stripe) * tag_width + LANES

        def body(s, carry, ref=ref, base=base):
            corner_row = tags[base + 2 * s]
            corner_col = tags[base + 2 * s + 1]
            offset = corner_row - stripe * stripe_rows
            keep = (rho >= offset) if keep_late else (rho < offset)
            piece = jnp.where(keep, ref[s], 0.0)
            block = corner_col >> 6
            ahead = jnp.where(kappa >= (corner_col & (SIDE - 1)), piece, 0.0)
            grid[block_at(block), :] += ahead
            grid[block_at((block + 1) & (blocks - 1)), :] += piece - ahead
            return carry

        lax.fori_loop(0, sub_count, body, 0, unroll=8)


def own_kernel(stripe_rows, tags, *refs):
    grid = refs[-1]
    grid[...] = jnp.zeros_like(grid)
    place(refs[:-1], stripe_rows, lax.axis_index("row"), True, tags, grid)


def spectrum_kernel(pieces, stripe_rows, tags, *refs):
    below = refs[:pieces]
    first, turn_c, turn_s, last, _, out, grid, ready, sent = refs[pieces:]
    rows = below[0].shape[1]
    pitch = odd_pitch(4 * rows)
    steps, out_rows = out.shape[1], out.shape[3] // 4
    out_pitch = odd_pitch(4 * out_rows)
    above = jnp.maximum(lax.axis_index("row") - 1, 0)
    place(below, stripe_rows, above, False, tags, grid)

    def pair(step, index):
        x = []
        for p in range(4):
            begin = p * rows + step * out_rows + 2 * index
            cols = jnp.concatenate(
                [grid[pl.ds(begin + e, QUARTER, stride=pitch), :] for e in range(2)], 1
            )
            high, low = split(cols)
            high = jnp.concatenate([high, turn(high)], 0)
            low = jnp.concatenate([low, turn(low)], 0)
            top = dot(first[p], high)
            x.append(top[:QUARTER] + top[QUARTER:] + dot(first[p, :QUARTER, :], low))
        a, b, c, d = x[0] + x[2], x[0] - x[2], x[1] + x[3], turn(x[1] - x[3])
        quarters = (a + c, b - d, a - c, b + d)
        for e in range(2):
            parts = []
            for h in range(4):
                y = quarters[h][:, e * LANES : (e + 1) * LANES]
                at = pl.ds(h * QUARTER, QUARTER)
                parts.append(y * turn_c[at, :] + pltpu.roll(y, SIDE, 1) * turn_s[at, :])
            high, low = split(jnp.concatenate(parts, 0))
            top = dot_nt(last[...], high)
            z = top[:LANES] + top[LANES:] + dot_nt(last[:LANES, :], low)
            for c in range(2):
                for q in range(4):
                    begin = q * out_rows + 2 * index + e
                    ready[step, c, pl.ds(begin, SIDE, stride=out_pitch), :] = z[
                        c * SIDE : (c + 1) * SIDE, q * LANES : (q + 1) * LANES
                    ]

    copies = []
    for step in range(steps):
        pairs = out_rows // 2
        lax.fori_loop(
            0, pairs, lambda n, carry, step=step: (pair(step, n), carry)[1], 0, unroll=True
        )
        for c in range(2):
            source = ready.at[step, c].reshape(SIDE, out_pitch, LANES)
            copies.append(
                pltpu.make_async_copy(
                    source.at[:, pl.ds(0, 4 * out_rows), :], out.at[c, step], sent.at[step, c]
                )
            )
            copies[-1].start()
    for copy in copies:
        copy.wait()


def local(
    visibilities, uv_cells, block_owner, block_subgrid, block_count, block_stations, corners, aterms
):
    tile_count = lax.axis_size("tile")
    row_count = lax.axis_size("row")
    owner_count = tile_count * row_count
    blocks_here = visibilities.shape[0]
    sub_count = corners.shape[0]
    stations = aterms.shape[0]
    capacity = max(2, 3 * blocks_here // owner_count)
    stride = max(8, 1 << (capacity + 1).bit_length())
    stripe_rows = SLAB // row_count
    piece_rows = stripe_rows // tile_count
    smem = pl.BlockSpec(memory_space=pltpu.SMEM)
    vmem = pl.BlockSpec(memory_space=pltpu.VMEM)

    message = pl.pallas_call(
        functools.partial(pack_kernel, capacity, stride),
        out_shape=jax.ShapeDtypeStruct((2 * owner_count * stride, LANES), jnp.float32),
        in_specs=[smem] * 5 + [vmem] * 2,
        out_specs=vmem,
        scratch_shapes=[pltpu.SMEM((owner_count,), jnp.int32)],
        name="pack",
    )(
        block_owner.reshape(-1),
        block_subgrid,
        block_count,
        block_stations.T,
        corners.T,
        visibilities,
        uv_cells,
    )
    got = lax.all_to_all(
        message.reshape(owner_count, 2, stride, LANES),
        ("tile", "row"),
        split_axis=0,
        concat_axis=0,
        tiled=True,
    )
    tags = got[:, :, capacity, :].astype(jnp.int32).reshape(-1)
    got = got.reshape(2 * owner_count * stride, LANES)

    line = aterms.shape[2] // LANES
    aterms = aterms.reshape(stations, 2, line, LANES).transpose(0, 2, 1, 3).reshape(-1, LANES)
    room = UNROLL * (owner_count * capacity // UNROLL + 1)
    anywhere = pl.BlockSpec(memory_space=pl.ANY)
    hbm = pl.BlockSpec(memory_space=pltpu.HBM)
    column, rows = (
        pltpu.with_memory_space_constraint(jnp.asarray(x), pltpu.HBM)
        for x in (np.stack(split_table(column_table())), row_table())
    )
    aterms = pltpu.with_memory_space_constraint(aterms, pltpu.HBM)
    patches = pl.pallas_call(
        functools.partial(grid_kernel, capacity, stride, tile_count),
        out_shape=[
            jax.ShapeDtypeStruct((sub_count, piece_rows, LANES), jnp.float32)
            for _ in range(tile_count)
        ],
        in_specs=[smem, vmem, hbm, hbm, hbm],
        out_specs=[vmem] * tile_count,
        scratch_shapes=[
            pltpu.VMEM((room, LANES), jnp.float32),
            pltpu.VMEM((room, LANES), jnp.float32),
            pltpu.VMEM((32 * room, LANES), jnp.float32),
            pltpu.VMEM((32 * room, LANES), jnp.float32),
            pltpu.VMEM((32 * room, LANES), jnp.float32),
            pltpu.VMEM((room, LANES), jnp.float32),
            pltpu.VMEM((room, LANES), jnp.float32),
            pltpu.VMEM((sub_count, SIDE, LANES), jnp.float32),
            pltpu.VMEM((max(2 * room, stations) * SIDE, LANES), aterms.dtype),
            pltpu.VMEM((2 * UNROLL * SIDE, LANES), jnp.float32),
            pltpu.VMEM((2, 4 * SIDE, 8 * SIDE), jnp.bfloat16),
            pltpu.VMEM((2 * SIDE, 2 * SIDE), jnp.float32),
            pltpu.SMEM((room + 8,), jnp.int32),
            pltpu.SemaphoreType.DMA((3,)),
            pltpu.SemaphoreType.DMA((room // UNROLL,)),
        ],
        compiler_params=pltpu.CompilerParams(vmem_limit_bytes=50 * 1024 * 1024),
        name="gridding",
    )(tags, got, aterms, column, rows)

    own, below = [], []
    down = [(i, i + 1) for i in range(row_count - 1)]
    for k in range(tile_count):
        piece = patches[k]
        if k > 0:
            piece = lax.ppermute(piece, "tile", [(i, (i + k) % tile_count) for i in range(tile_count)])
        own.append(piece)
        below.append(lax.ppermute(piece, "row", down))

    turn_c, turn_s = twiddle_tables()
    out_rows = min(8, piece_rows)
    steps = piece_rows // out_rows
    grid_shape = pltpu.VMEM((QUARTER * odd_pitch(4 * piece_rows), LANES), jnp.float32)
    grid = pl.pallas_call(
        functools.partial(own_kernel, stripe_rows),
        out_shape=grid_shape,
        in_specs=[smem] + [vmem] * tile_count,
        out_specs=vmem,
        compiler_params=pltpu.CompilerParams(vmem_limit_bytes=4 * 1024 * 1024),
        name="place_own",
    )(tags, *own)
    grid = pltpu.with_memory_space_constraint(grid, pltpu.VMEM)
    spectrum, _ = pl.pallas_call(
        functools.partial(spectrum_kernel, tile_count, stripe_rows),
        out_shape=[
            jax.ShapeDtypeStruct((2, steps, SIDE, 4 * out_rows, LANES), jnp.float32),
            grid_shape,
        ],
        in_specs=[smem] + [vmem] * (tile_count + 5),
        out_specs=[anywhere, vmem],
        input_output_aliases={tile_count + 5: 1},
        scratch_shapes=[
            pltpu.VMEM((steps, 2, SIDE * odd_pitch(4 * out_rows), LANES), jnp.float32),
            pltpu.SemaphoreType.DMA((steps, 2)),
        ],
        compiler_params=pltpu.CompilerParams(vmem_limit_bytes=32 * 1024 * 1024),
        name="spectrum",
    )(tags, *below, stage_table(), turn_c, turn_s, last_table(), grid)
    spectrum = spectrum.reshape(2, steps, GRID // LANES, out_rows, LANES).transpose(0, 1, 3, 2, 4)
    return spectrum.reshape(2, 1, piece_rows, GRID)


def solution(mesh):
    in_specs = (
        P(("groups", "tile", "row"), None),
        P(("groups", "tile", "row"), None),
        P(("groups", "tile", "row"), None),
        P(("groups", "tile", "row")),
        P(("groups", "tile", "row")),
        P(("groups", "tile", "row"), None),
        P(("groups", "tile", "row"), None),
        P(),
    )
    out_specs = P(None, ("groups", "row"), "tile", None)
    return jax.shard_map(local, mesh=mesh, in_specs=in_specs, out_specs=out_specs, check_vma=False)
```

```python
import functools
import math

import jax
import jax.numpy as jnp
import numpy as np
from jax import lax
from jax.experimental import pallas as pl
from jax.experimental.pallas import tpu as pltpu
from jax.sharding import PartitionSpec as P

GRID = 32768
SLAB = 256
SIDE = 64
LANES = 128
UNROLL = 16
QUARTER = GRID // SIDE // 4

SIN_TERMS = (
    6.2831852724479385, -41.3416970381994, 81.60502363801741, -76.70153767001833,
    42.01607576032372, -14.868322746301509, 3.199338837237415,
)
COS_TERMS = (
    0.9999999890590211, -19.73920449945394, 64.93911745989672, -85.45013953089433,
    60.167630950968515, -25.967599248305554, 6.528658160795414,
)


def poly(terms, z):
    total = jnp.full_like(z, terms[-1])
    for term in terms[-2::-1]:
        total = total * z + term
    return total


def cos_sin(turns):
    rest = turns - jnp.round(turns)
    z = rest * rest
    return poly(COS_TERMS, z), rest * poly(SIN_TERMS, z)


def split(x):
    high = x.astype(jnp.bfloat16)
    return high, (x - high.astype(jnp.float32)).astype(jnp.bfloat16)


def split_table(table):
    high = table.astype(jnp.bfloat16)
    return high, (table - high.astype(np.float64)).astype(jnp.bfloat16)


def dot(a, b):
    return jnp.dot(a, b, preferred_element_type=jnp.float32)


def dot_nt(a, b):
    return lax.dot_general(a, b, (((1,), (1,)), ((), ())), preferred_element_type=jnp.float32)


def taper():
    edge = (2.0 * np.arange(SIDE) + 1.0) / SIDE - 1.0
    return 1.0 - 0.9 * edge * edge


def column_table():
    m = np.arange(SIDE)
    angle = 2.0 * np.pi * (m[:, None] * m[None, :] % SIDE) / SIDE
    scale = 1.0 / (SIDE * math.sqrt(SIDE) * math.sqrt(GRID))
    real = scale * taper()[:, None] * np.cos(angle)
    imag = -scale * taper()[:, None] * np.sin(angle)
    table = np.zeros((2, 2, SIDE, 2, 2, 2, SIDE))
    for p in range(2):
        table[0, p, :, 0, p, 0] = real
        table[0, p, :, 0, p, 1] = imag
        table[1, p, :, 0, p, 0] = -imag
        table[1, p, :, 0, p, 1] = real
        table[0, p, :, 1, p, 0] = -imag
        table[0, p, :, 1, p, 1] = real
        table[1, p, :, 1, p, 0] = -real
        table[1, p, :, 1, p, 1] = -imag
    return table.reshape(4 * SIDE, 8 * SIDE)


def row_table():
    rho = np.arange(2 * SIDE) % SIDE
    a = np.arange(SIDE // 2)
    blocks = []
    for kind in (np.cos, lambda t: -np.sin(t)):
        for p in range(2):
            l = 2 * a + p
            blocks.append(taper()[l][None, :] * kind(2.0 * np.pi * (rho[:, None] * l[None, :] % SIDE) / SIDE))
    return np.concatenate(blocks, 1).astype(np.float32)


def stage_table():
    k = np.arange(QUARTER)[:, None]
    t = np.arange(QUARTER)[None, :]
    out = []
    for p in range(4):
        angle = 2.0 * np.pi * (k * (4 * t + p) % (4 * QUARTER)) / (4 * QUARTER)
        high, low = split_table(np.concatenate([np.cos(angle), -np.sin(angle)], 1))
        out.append(np.concatenate([high, low], 0))
    return np.stack(out)


def twiddle_tables():
    k = np.arange(4 * QUARTER)[:, None]
    kappa = np.arange(SIDE)[None, :]
    angle = 2.0 * np.pi * (k * kappa % GRID) / GRID
    c, s = np.cos(angle), np.sin(angle)
    return (
        np.concatenate([c, c], 1).astype(np.float32),
        np.concatenate([s, -s], 1).astype(np.float32),
    )


def last_table():
    k = np.arange(SIDE)[:, None]
    kappa = np.arange(SIDE)[None, :]
    angle = 2.0 * np.pi * (k * kappa % SIDE) / SIDE
    c, s = np.cos(angle), np.sin(angle)
    high, low = split_table(np.block([[c, s], [-s, c]]))
    return np.concatenate([high, low], 0)


def pack_kernel(capacity, stride, owner, sub, count, stations, corners, vis, uv, message, used):
    owners = message.shape[0] // (2 * stride)
    blocks = vis.shape[0]
    lane = lax.broadcasted_iota(jnp.int32, (1, LANES), 1)
    message[...] = jnp.zeros_like(message)

    def corner(i, row):
        for c in range(2):
            row = jnp.where(lane == 2 * i + c, corners[c, i].astype(jnp.float32), row)
        return row

    corner_row = lax.fori_loop(
        0, corners.shape[1], corner, jnp.zeros((1, LANES), jnp.float32), unroll=True
    )

    def clear(o, carry):
        used[o] = 0
        message[pl.ds((2 * o + 1) * stride + capacity, 1), :] = corner_row
        return carry

    lax.fori_loop(0, owners, clear, 0, unroll=8)

    k_at = lane & (SIDE - 1)

    def place(g, carry):
        o = owner[g]
        slot = used[o]
        used[o] = slot + 1
        row = 2 * o * stride + slot
        live = k_at < count[g]
        message[pl.ds(row, 1), :] = jnp.where(live, vis[pl.ds(g, 1), :], 0.0)
        message[pl.ds(row + stride, 1), :] = uv[pl.ds(g, 1), :]
        tags_at = pl.ds(2 * o * stride + capacity, 1)
        tag_row = message[tags_at, :]
        at = 4 * slot
        for i, value in enumerate((sub[g], count[g], stations[0, g], stations[1, g])):
            tag_row = jnp.where(lane == at + i, value.astype(jnp.float32), tag_row)
        message[tags_at, :] = tag_row
        return carry

    lax.fori_loop(0, blocks, place, 0, unroll=16)


def grid_kernel(
    capacity, stride, pieces, tags, got, aterms, col, rows, *refs
):
    outs, (rows_v, rows_uv, left, right_re, right_im, two_u, two_v, subgrids, raw, gains, col_here, rows_here, listed, arrived, gained) = (
        refs[:pieces],
        refs[pieces:],
    )
    owners = got.shape[0] // (2 * stride)
    shift = (2 * stride).bit_length() - 1
    sub_count = outs[0].shape[0]
    piece_rows = outs[0].shape[1]
    room = rows_v.shape[0]
    lane = lax.broadcasted_iota(jnp.int32, (1, LANES), 1)
    low = lane < SIDE
    tag_width = 2 * LANES
    tile_at, row_at = lax.axis_index("tile"), lax.axis_index("row")
    mine = (tile_at * lax.axis_size("row") + row_at) * tag_width + LANES

    stations = aterms.shape[0] // SIDE
    loads = [
        pltpu.make_async_copy(col, col_here, arrived.at[0]),
        pltpu.make_async_copy(rows, rows_here, arrived.at[1]),
        pltpu.make_async_copy(aterms, raw.at[pl.ds(0, stations * SIDE)], arrived.at[2]),
    ]
    for load in loads[:2]:
        load.start()
    subgrids[...] = jnp.zeros_like(subgrids)

    def collect(source, found):
        for c in range(capacity):
            listed[found] = 2 * source * stride + c
            found = found + (tags[source * tag_width + 4 * c + 1] > 0).astype(jnp.int32)
        return found

    total = lax.fori_loop(0, owners, collect, jnp.int32(0))
    for i in range(UNROLL):
        listed[total + i] = capacity + 1
    many = total > stations // 4

    @pl.when(many)
    def _():
        loads[2].start()

    def fetch_gains(group, carry):
        for e in range(UNROLL):
            at = group * UNROLL + e
            entry = listed[at]
            tag = (entry >> shift) * tag_width + 4 * (entry & (stride - 1))
            for i in range(2):
                begin = pl.multiple_of(tags[tag + 2 + i] * SIDE, SIDE)
                pltpu.make_async_copy(
                    aterms.at[pl.ds(begin, SIDE)],
                    raw.at[pl.ds(pl.multiple_of((2 * at + i) * SIDE, SIDE), SIDE)],
                    gained.at[group],
                ).start()
        return carry

    def fetch(n):
        for e in range(8):
            at = n * 8 + e
            entry = listed[at]
            source, c = entry >> shift, entry & (stride - 1)
            tag = source * tag_width + 4 * c
            sub = tags[tag]
            shift_u = (tags[mine + 2 * sub] & (SIDE - 1)).astype(jnp.float32)
            shift_v = (tags[mine + 2 * sub + 1] & (SIDE - 1)).astype(jnp.float32)
            rows_v[pl.ds(at, 1), :] = got[pl.ds(entry, 1), :]
            rows_uv[pl.ds(at, 1), :] = got[pl.ds(entry + stride, 1), :] + jnp.where(low, shift_u, shift_v)
        base = pl.multiple_of(n * 8, 8)
        v = rows_v[pl.ds(base, 8), :]
        turns = rows_uv[pl.ds(base, 8), :] * (1.0 / SIDE)
        c1, s1 = cos_sin(turns)
        c16, s16 = cos_sin(turns * 16.0)
        rc1, rs1 = pltpu.roll(c1, SIDE, 1), pltpu.roll(s1, SIDE, 1)
        rc16, rs16 = pltpu.roll(c16, SIDE, 1), pltpu.roll(s16, SIDE, 1)
        cu, su = jnp.where(low, c1, rc1), jnp.where(low, s1, rs1)
        cv, sv = jnp.where(low, rc1, c1), jnp.where(low, rs1, s1)
        cu16, su16 = jnp.where(low, c16, rc16), jnp.where(low, s16, rs16)
        cv16, sv16 = jnp.where(low, rc16, c16), jnp.where(low, rs16, s16)
        two_u[pl.ds(base, 8), :] = 2.0 * cu16
        two_v[pl.ds(base, 8), :] = 2.0 * cv16
        a = v
        b = pltpu.roll(v, SIDE, 1) * jnp.where(low, -1.0, 1.0)
        x = jnp.broadcast_to(jnp.where(low, 1.0, 0.0), v.shape)
        y = jnp.broadcast_to(jnp.where(low, 0.0, 1.0), v.shape)
        for l in range(16):
            left[pl.ds(l * room + base, 8), :] = a
            left[pl.ds((l + 16) * room + base, 8), :] = a * cu16 + b * su16
            right_re[pl.ds(l * room + base, 8), :] = x
            right_im[pl.ds(l * room + base, 8), :] = y
            right_re[pl.ds((l + 16) * room + base, 8), :] = x * cv16 - y * sv16
            right_im[pl.ds((l + 16) * room + base, 8), :] = y * cv16 + x * sv16
            if l < 15:
                a, b = a * cu + b * su, b * cu - a * su
                x, y = x * cv - y * sv, y * cv + x * sv
    groups = (total + UNROLL - 1) // UNROLL

    def fetch_group(group, carry):
        for i in range(UNROLL // 8):
            fetch(group * (UNROLL // 8) + i)
        return carry

    lax.fori_loop(0, jnp.where(many, 0, groups), fetch_gains, 0)
    lax.fori_loop(0, groups, fetch_group, 0)

    @pl.when(many)
    def _():
        loads[2].wait()

    def image(at):
        ku = two_u[pl.ds(at, 1), :]
        kv = two_v[pl.ds(at, 1), :]
        ls = []
        for p in range(2):
            chain = [left[pl.ds((16 * j + p) * room + at, 8, stride=2 * room), :] for j in range(2)]
            for j in range(2):
                chain.append(ku * chain[-1] - chain[-2])
            ls.extend(chain)
        sides = []
        for ref in (right_re, right_im):
            chain = [ref[pl.ds(8 * q * room + at, 8, stride=room), :] for q in range(4)]
            for q in range(4):
                chain.append(kv * chain[-2] - chain[-4])
            sides.append(jnp.concatenate(chain, 0))
        l_high, l_low = split(jnp.concatenate(ls, 0))
        re_high, re_low = split(sides[0])
        im_high, im_low = split(sides[1])
        r_high = jnp.concatenate([re_high, im_high], 0)
        r_low = jnp.concatenate([re_low, im_low], 0)
        top = dot_nt(jnp.concatenate([l_high, l_low], 0), r_high)
        both = top[:SIDE] + top[SIDE:] + dot_nt(l_high, r_low)
        half = SIDE // 2
        even, odd = both[:half], both[half:]
        re = jnp.where(low, even, pltpu.roll(odd, SIDE, 1))
        im = jnp.where(low, pltpu.roll(even, SIDE, 1), odd)
        return re, im

    span = 2 * UNROLL * SIDE

    def weigh(turn, carry):
        half = SIDE // 2
        begin = pl.multiple_of(turn * span, span)

        @pl.when(jnp.logical_not(many))
        def _():
            pltpu.make_async_copy(
                aterms.at[pl.ds(0, span)], raw.at[pl.ds(begin, span)], gained.at[turn]
            ).wait()

        for e in range(UNROLL):
            at = turn * UNROLL + e
            entry = listed[at]
            tag = (entry >> shift) * tag_width + 4 * (entry & (stride - 1))
            for i in range(2):
                row = pl.multiple_of(
                    jnp.where(many, tags[tag + 2 + i] * SIDE, (2 * at + i) * SIDE), SIDE
                )
                gains[(2 * e + i) * SIDE : (2 * e + i + 1) * SIDE, :] = raw[
                    pl.ds(row, SIDE), :
                ].astype(jnp.float32)
        images = [image(turn * UNROLL + e) for e in range(UNROLL)]
        for e in range(UNROLL):
            at = turn * UNROLL + e
            entry = listed[at]
            source, c = entry >> shift, entry & (stride - 1)
            tag = source * tag_width + 4 * c
            sub = tags[tag]
            re, im = images[e]
            pr, pi = (gains[pl.ds(2 * e * SIDE + i, half, stride=2), :] for i in range(2))
            qr, qi = (gains[pl.ds((2 * e + 1) * SIDE + i, half, stride=2), :] for i in range(2))
            fr = pr * qr + pi * qi
            fi = pi * qr - pr * qi
            subgrids[sub, :half, :] += re * fr - im * fi
            subgrids[sub, half:, :] += re * fi + im * fr
        return carry

    lax.fori_loop(0, groups, weigh, 0)

    loads[0].wait()
    loads[1].wait()
    batch = min(8, sub_count)
    table_high, table_low = split(rows_here[pl.ds(tile_at * piece_rows, SIDE), :])
    table = jnp.concatenate([table_high, table_low], 0)

    def transform(turn, carry):
        half = SIDE // 2
        first = turn * batch
        data = []
        for e in range(batch):
            both = subgrids[first + e]
            data.append(jnp.concatenate([both[:half], both[half:]], 1))
        d_high, d_low = split(jnp.concatenate(data, 0))
        mid = dot(d_high, col_here[0]) + dot(d_low, col_here[0]) + dot(d_high, col_here[1])
        for e in range(0, batch, 2):
            stack = []
            for part in (mid[e * half : (e + 1) * half], mid[(e + 1) * half : (e + 2) * half]):
                stack.append(jnp.concatenate([part[:, q * LANES : (q + 1) * LANES] for q in range(4)], 0))
            s_high, s_low = split(jnp.concatenate(stack, 1))
            top = dot(table, s_high)
            patch = top[:SIDE] + top[SIDE:] + dot(table_high, s_low)
            for k in range(pieces):
                for i in range(2):
                    outs[k][first + e + i] = patch[k * piece_rows : (k + 1) * piece_rows, i * LANES : (i + 1) * LANES]
        return carry

    lax.fori_loop(0, sub_count // batch, transform, 0, unroll=True)


def turn(x):
    sign = jnp.where(lax.broadcasted_iota(jnp.int32, (1, LANES), 1) < SIDE, -1.0, 1.0)
    tiles = [x[:, i : i + LANES] for i in range(0, x.shape[1], LANES)]
    return jnp.concatenate([pltpu.roll(tile, SIDE, 1) * sign for tile in tiles], 1)


def odd_pitch(rows):
    return rows + 8 * (rows // 8 % 2 == 0)


def place(pieces, stripe_rows, stripe, keep_late, tags, grid):
    sub_count, rows, _ = pieces[0].shape
    tag_width = 2 * LANES
    blocks = 4 * QUARTER
    pitch = odd_pitch(4 * rows)
    tile_at = lax.axis_index("tile")
    row_count = lax.axis_size("row")
    kappa = lax.broadcasted_iota(jnp.int32, (rows, LANES), 1) % SIDE
    rho = lax.broadcasted_iota(jnp.int32, (rows, LANES), 0) + rows * tile_at

    def block_at(block):
        begin = (block >> 2) * pitch + (block & 3) * rows
        return pl.ds(pl.multiple_of(begin, math.gcd(rows, 8)), rows)

    for k, ref in enumerate(pieces):
        source = (tile_at - k + len(pieces)) % len(pieces)
        base = (source * row_count + stripe) * tag_width + LANES

        def body(s, carry, ref=ref, base=base):
            corner_row = tags[base + 2 * s]
            corner_col = tags[base + 2 * s + 1]
            offset = corner_row - stripe * stripe_rows
            keep = (rho >= offset) if keep_late else (rho < offset)
            piece = jnp.where(keep, ref[s], 0.0)
            block = corner_col >> 6
            ahead = jnp.where(kappa >= (corner_col & (SIDE - 1)), piece, 0.0)
            grid[block_at(block), :] += ahead
            grid[block_at((block + 1) & (blocks - 1)), :] += piece - ahead
            return carry

        lax.fori_loop(0, sub_count, body, 0, unroll=8)


def own_kernel(stripe_rows, tags, *refs):
    grid = refs[-1]
    grid[...] = jnp.zeros_like(grid)
    place(refs[:-1], stripe_rows, lax.axis_index("row"), True, tags, grid)


def spectrum_kernel(pieces, stripe_rows, tags, *refs):
    below = refs[:pieces]
    first, turn_c, turn_s, last, _, out, grid, ready, sent = refs[pieces:]
    rows = below[0].shape[1]
    pitch = odd_pitch(4 * rows)
    steps, out_rows = out.shape[1], out.shape[3] // 4
    out_pitch = odd_pitch(4 * out_rows)
    above = jnp.maximum(lax.axis_index("row") - 1, 0)
    place(below, stripe_rows, above, False, tags, grid)

    def pair(step, index):
        x = []
        for p in range(4):
            begin = p * rows + step * out_rows + 2 * index
            cols = jnp.concatenate(
                [grid[pl.ds(begin + e, QUARTER, stride=pitch), :] for e in range(2)], 1
            )
            high, low = split(cols)
            high = jnp.concatenate([high, turn(high)], 0)
            low = jnp.concatenate([low, turn(low)], 0)
            top = dot(first[p], high)
            x.append(top[:QUARTER] + top[QUARTER:] + dot(first[p, :QUARTER, :], low))
        a, b, c, d = x[0] + x[2], x[0] - x[2], x[1] + x[3], turn(x[1] - x[3])
        quarters = (a + c, b - d, a - c, b + d)
        for e in range(2):
            parts = []
            for h in range(4):
                y = quarters[h][:, e * LANES : (e + 1) * LANES]
                at = pl.ds(h * QUARTER, QUARTER)
                parts.append(y * turn_c[at, :] + pltpu.roll(y, SIDE, 1) * turn_s[at, :])
            high, low = split(jnp.concatenate(parts, 0))
            top = dot_nt(last[...], high)
            z = top[:LANES] + top[LANES:] + dot_nt(last[:LANES, :], low)
            for c in range(2):
                for q in range(4):
                    begin = q * out_rows + 2 * index + e
                    ready[step, c, pl.ds(begin, SIDE, stride=out_pitch), :] = z[
                        c * SIDE : (c + 1) * SIDE, q * LANES : (q + 1) * LANES
                    ]

    copies = []
    for step in range(steps):
        pairs = out_rows // 2
        lax.fori_loop(
            0, pairs, lambda n, carry, step=step: (pair(step, n), carry)[1], 0, unroll=True
        )
        for c in range(2):
            source = ready.at[step, c].reshape(SIDE, out_pitch, LANES)
            copies.append(
                pltpu.make_async_copy(
                    source.at[:, pl.ds(0, 4 * out_rows), :], out.at[c, step], sent.at[step, c]
                )
            )
            copies[-1].start()
    for copy in copies:
        copy.wait()


def local(
    visibilities, uv_cells, block_owner, block_subgrid, block_count, block_stations, corners, aterms
):
    tile_count = lax.axis_size("tile")
    row_count = lax.axis_size("row")
    owner_count = tile_count * row_count
    blocks_here = visibilities.shape[0]
    sub_count = corners.shape[0]
    stations = aterms.shape[0]
    capacity = max(2, 3 * blocks_here // owner_count)
    stride = max(8, 1 << (capacity + 1).bit_length())
    stripe_rows = SLAB // row_count
    piece_rows = stripe_rows // tile_count
    smem = pl.BlockSpec(memory_space=pltpu.SMEM)
    vmem = pl.BlockSpec(memory_space=pltpu.VMEM)

    message = pl.pallas_call(
        functools.partial(pack_kernel, capacity, stride),
        out_shape=jax.ShapeDtypeStruct((2 * owner_count * stride, LANES), jnp.float32),
        in_specs=[smem] * 5 + [vmem] * 2,
        out_specs=vmem,
        scratch_shapes=[pltpu.SMEM((owner_count,), jnp.int32)],
        name="pack",
    )(
        block_owner.reshape(-1),
        block_subgrid,
        block_count,
        block_stations.T,
        corners.T,
        visibilities,
        uv_cells,
    )
    got = lax.all_to_all(
        message.reshape(owner_count, 2, stride, LANES),
        ("tile", "row"),
        split_axis=0,
        concat_axis=0,
        tiled=True,
    )
    tags = got[:, :, capacity, :].astype(jnp.int32).reshape(-1)
    got = got.reshape(2 * owner_count * stride, LANES)

    line = aterms.shape[2] // LANES
    aterms = aterms.reshape(stations, 2, line, LANES).transpose(0, 2, 1, 3).reshape(-1, LANES)
    room = UNROLL * (owner_count * capacity // UNROLL + 1)
    anywhere = pl.BlockSpec(memory_space=pl.ANY)
    hbm = pl.BlockSpec(memory_space=pltpu.HBM)
    column, rows = (
        pltpu.with_memory_space_constraint(jnp.asarray(x), pltpu.HBM)
        for x in (np.stack(split_table(column_table())), row_table())
    )
    aterms = pltpu.with_memory_space_constraint(aterms, pltpu.HBM)
    patches = pl.pallas_call(
        functools.partial(grid_kernel, capacity, stride, tile_count),
        out_shape=[
            jax.ShapeDtypeStruct((sub_count, piece_rows, LANES), jnp.float32)
            for _ in range(tile_count)
        ],
        in_specs=[smem, vmem, hbm, hbm, hbm],
        out_specs=[vmem] * tile_count,
        scratch_shapes=[
            pltpu.VMEM((room, LANES), jnp.float32),
            pltpu.VMEM((room, LANES), jnp.float32),
            pltpu.VMEM((32 * room, LANES), jnp.float32),
            pltpu.VMEM((32 * room, LANES), jnp.float32),
            pltpu.VMEM((32 * room, LANES), jnp.float32),
            pltpu.VMEM((room, LANES), jnp.float32),
            pltpu.VMEM((room, LANES), jnp.float32),
            pltpu.VMEM((sub_count, SIDE, LANES), jnp.float32),
            pltpu.VMEM((max(2 * room, stations) * SIDE, LANES), aterms.dtype),
            pltpu.VMEM((2 * UNROLL * SIDE, LANES), jnp.float32),
            pltpu.VMEM((2, 4 * SIDE, 8 * SIDE), jnp.bfloat16),
            pltpu.VMEM((2 * SIDE, 2 * SIDE), jnp.float32),
            pltpu.SMEM((room + 8,), jnp.int32),
            pltpu.SemaphoreType.DMA((3,)),
            pltpu.SemaphoreType.DMA((room // UNROLL,)),
        ],
        compiler_params=pltpu.CompilerParams(vmem_limit_bytes=50 * 1024 * 1024),
        name="gridding",
    )(tags, got, aterms, column, rows)

    own, below = [], []
    down = [(i, i + 1) for i in range(row_count - 1)]
    for k in range(tile_count):
        piece = patches[k]
        if k > 0:
            piece = lax.ppermute(piece, "tile", [(i, (i + k) % tile_count) for i in range(tile_count)])
        own.append(piece)
        below.append(lax.ppermute(piece, "row", down))

    turn_c, turn_s = twiddle_tables()
    out_rows = min(8, piece_rows)
    steps = piece_rows // out_rows
    grid_shape = pltpu.VMEM((QUARTER * odd_pitch(4 * piece_rows), LANES), jnp.float32)
    grid = pl.pallas_call(
        functools.partial(own_kernel, stripe_rows),
        out_shape=grid_shape,
        in_specs=[smem] + [vmem] * tile_count,
        out_specs=vmem,
        compiler_params=pltpu.CompilerParams(vmem_limit_bytes=4 * 1024 * 1024),
        name="place_own",
    )(tags, *own)
    grid = pltpu.with_memory_space_constraint(grid, pltpu.VMEM)
    spectrum, _ = pl.pallas_call(
        functools.partial(spectrum_kernel, tile_count, stripe_rows),
        out_shape=[
            jax.ShapeDtypeStruct((2, steps, SIDE, 4 * out_rows, LANES), jnp.float32),
            grid_shape,
        ],
        in_specs=[smem] + [vmem] * (tile_count + 5),
        out_specs=[anywhere, vmem],
        input_output_aliases={tile_count + 5: 1},
        scratch_shapes=[
            pltpu.VMEM((steps, 2, SIDE * odd_pitch(4 * out_rows), LANES), jnp.float32),
            pltpu.SemaphoreType.DMA((steps, 2)),
        ],
        compiler_params=pltpu.CompilerParams(vmem_limit_bytes=32 * 1024 * 1024),
        name="spectrum",
    )(tags, *below, stage_table(), turn_c, turn_s, last_table(), grid)
    spectrum = spectrum.reshape(2, steps, GRID // LANES, out_rows, LANES).transpose(0, 1, 3, 2, 4)
    return spectrum.reshape(2, 1, piece_rows, GRID)


def solution(mesh):
    in_specs = (
        P(("groups", "tile", "row"), None),
        P(("groups", "tile", "row"), None),
        P(("groups", "tile", "row"), None),
        P(("groups", "tile", "row")),
        P(("groups", "tile", "row")),
        P(("groups", "tile", "row"), None),
        P(("groups", "tile", "row"), None),
        P(),
    )
    out_specs = P(None, ("groups", "row"), "tile", None)
    return jax.shard_map(local, mesh=mesh, in_specs=in_specs, out_specs=out_specs, check_vma=False)
```
